32 devices in a mesh: segment: 4 (over y, x), ctx: 4 (over z), tp: 2 (over core).
Axes of the slice: x: 2, y: 2, z: 4, core: 2. Of those that a mesh axis runs over, the one named last changes fastest.
Arguments:
- mamba_input: bfloat16 [4, 512, 8192], P('segment', 'ctx', 'tp'), may hold values from -13 to 13
- mamba_gate: bfloat16 [4, 512, 8192], P('segment', 'ctx', 'tp'), may hold values from -6 to 6
- step_size: bfloat16 [4, 512, 128], P('segment', 'ctx', 'tp'), may hold values from 0 to 2, as said below
- state_maps: bfloat16 [4, 512, 256], P('segment', 'ctx'), may hold values from -3 to 3
- decay_rate: float32 [128], P('tp'), may hold values from 0.5 to 2
- skip_gain: float32 [128], P('tp'), may hold values from 0.5 to 1.5
- norm_gain: float32 [8192], P('tp'), may hold values from 0.1 to 1.9
- queries: bfloat16 [4, 512, 8192], P('segment', 'ctx', 'tp'), may hold values from -155 to 154
- keys: bfloat16 [4, 512, 1024], P('segment', 'ctx', 'tp'), may hold values from -5 to 5
- values: bfloat16 [4, 512, 1024], P('segment', 'ctx', 'tp'), may hold values from -6 to 6
- source_len: int32 [4], P('segment'), may hold values from 204 to 459
Outputs:
- mamba_handed: bfloat16 [4, 512, 8192], P('segment', 'ctx', 'tp')
- attention_handed: bfloat16 [4, 512, 8192], P('segment', 'ctx', 'tp')
The draws below stay inside these ranges and needn't reach their ends.
Inputs may be any that keep to these rules, and one draw needn't show every extreme that they name: `step_size`: positive.
All inputs are finite; a program needn't handle non-finite values.
Results may differ from the reference program's by a relative error of at most 0.0095.
Values may be sent and summed in bfloat16 or wider, within the bound.
No kernel may reach another device: no remote copies, remote signals or barrier semaphores. Data moves between devices by JAX's collectives and lax.ppermute only.
A program may use at most 320 MiB of HBM per device.

```python
import math
import jax
import jax.numpy as jnp
from jax import lax

QUERY_HEADS = 64
KEY_VALUE_HEADS = 8
HEAD_WIDTH = 128
NST = 128
EM = 8192
HP = 64
MH = 128
MICRO_BATCHES = 4
SEQUENCE_TOKENS = 512


def head_kinds(key):
    share = 4
    return jax.random.randint(jax.random.fold_in(key, 11), (MH,), 0, 8) < share


def rate_values(key):
    return jnp.exp(jax.random.uniform(jax.random.fold_in(key, 21), (MH,), jnp.float32, math.log(0.5), math.log(2.0)))


def draw_decay_rate(key, part):
    return rate_values(key)


def draw_step_size(key, part):
    speed_collection = rate_values(key)
    quick_route = head_kinds(key)
    rough = jnp.exp(jax.random.uniform(jax.random.fold_in(key, 31), (MICRO_BATCHES, SEQUENCE_TOKENS, MH), jnp.float32, math.log(0.5), math.log(2.0)))
    per_quick = jnp.exp(jax.random.uniform(jax.random.fold_in(key, 32), (MH,), jnp.float32, math.log(1.0 / 50.0), math.log(1.0 / 30.0)))
    whole_loss = jnp.exp(jax.random.uniform(jax.random.fold_in(key, 33), (MH,), jnp.float32, math.log(2.0), math.log(5.0)))
    base = jnp.where(quick_route, per_quick / speed_collection, whole_loss / (SEQUENCE_TOKENS * speed_collection))
    increment_collection = base[None, None, :] * rough
    spots = jax.random.randint(jax.random.fold_in(key, 34), (MICRO_BATCHES, 3, MH), 0, SEQUENCE_TOKENS)
    places = jnp.arange(SEQUENCE_TOKENS, dtype=jnp.int32)
    masked_indicators = jnp.any(places[None, :, None, None] == spots[:, None, :, :], axis=2)
    blend_coefficient = jax.random.uniform(jax.random.fold_in(key, 35), (MICRO_BATCHES, SEQUENCE_TOKENS, MH), jnp.float32, 0.22, 0.51)
    spike_collection = blend_coefficient / speed_collection[None, None, :]
    increment_collection = jnp.where(masked_indicators & jnp.logical_not(quick_route)[None, None, :], spike_collection, increment_collection)
    return increment_collection.astype(jnp.bfloat16)


def draw_mamba_input(key, part):
    channel = jnp.arange(EM, dtype=jnp.float32) / (EM - 1)
    spread = jnp.exp(jax.random.uniform(jax.random.fold_in(key, 52), (EM,), jnp.float32, math.log(0.7), math.log(1.4)))
    base = jnp.clip(jax.random.normal(jax.random.fold_in(key, 51), (MICRO_BATCHES, SEQUENCE_TOKENS, EM), jnp.float32), -5.0, 5.0)
    ramp = 0.6 * jnp.power(3.0, channel)
    return (base * ramp[None, None, :] * spread[None, None, :]).astype(jnp.bfloat16)


def attention_draw(key):
    query_base = jnp.clip(jax.random.normal(jax.random.fold_in(key, 41), (MICRO_BATCHES, SEQUENCE_TOKENS, QUERY_HEADS * HEAD_WIDTH), jnp.float32), -5.0, 5.0)
    key_offset = jnp.clip(jax.random.normal(jax.random.fold_in(key, 42), (MICRO_BATCHES, SEQUENCE_TOKENS, KEY_VALUE_HEADS * HEAD_WIDTH), jnp.float32), -5.0, 5.0)
    return (query_base, key_offset)


def draw_queries(key, part):
    return attention_draw(key)[0].astype(jnp.bfloat16)


def draw_keys(key, part):
    return attention_draw(key)[1].astype(jnp.bfloat16)


def with_ends(result, key, low, largest):
    extent = result.shape
    index_at = [jax.random.randint(jax.random.fold_in(key, axis), (), 0, extent[axis]) for axis in range(len(extent))]
    result = result.at[tuple(index_at)].set(low)
    longest = extent.index(max(extent))
    index_at[longest] = (index_at[longest] + 1) % extent[longest]
    return result.at[tuple(index_at)].set(largest)


def block_levels(rng, extent, shards, smallest, top_value):
    loudness = 1.0
    for dim, shards_of in shards:
        heights = jax.random.uniform(jax.random.fold_in(jax.random.fold_in(rng, 6), dim), (shards_of,), jnp.float32, smallest / len(shards), top_value / len(shards))
        loudness = loudness * jnp.repeat(jnp.exp(heights), extent[dim] // shards_of).reshape((-1,) + (1,) * (len(extent) - 1 - dim))
    return loudness


def noise(key, extent, width, most, shards=(), kind=jnp.bfloat16):
    array = jax.random.normal(key, extent, jnp.float32) * width
    if len(shards) > 0:
        array = block_levels(key, extent, shards, -0.22, 0.18) * array
    return jnp.clip(array, min=-most, max=most).astype(kind)


def setup_inputs(seed: int = 0) -> dict:
    arg_keys = jax.random.split(jax.random.key(seed), 12)
    return {
        "mamba_input": draw_mamba_input(jax.random.fold_in(arg_keys[11], 71), 0),
        "mamba_gate": noise(arg_keys[1], (MICRO_BATCHES, SEQUENCE_TOKENS, EM), 1.0, 6.0, ((0, 4), (1, 4), (2, 2))),
        "step_size": draw_step_size(jax.random.fold_in(arg_keys[11], 71), 0),
        "state_maps": noise(arg_keys[3], (MICRO_BATCHES, SEQUENCE_TOKENS, 2 * NST), 0.6, 3.0, ((0, 4), (1, 4))),
        "decay_rate": draw_decay_rate(jax.random.fold_in(arg_keys[11], 71), 0),
        "skip_gain": jnp.clip(jnp.exp(math.log(1.5) - 1.0986123 * jax.random.uniform(arg_keys[5], (MH,), jnp.float32) ** block_levels(arg_keys[5], (MH,), ((0, 2),), -0.2, 0.2)), 0.5, 1.5),
        "norm_gain": jnp.clip(1.0 + 0.18 * jax.random.normal(arg_keys[6], (EM,), jnp.float32), 0.1, 1.9),
        "queries": draw_queries(jax.random.fold_in(arg_keys[11], 71), 0),
        "keys": draw_keys(jax.random.fold_in(arg_keys[11], 71), 0),
        "values": noise(arg_keys[9], (MICRO_BATCHES, SEQUENCE_TOKENS, KEY_VALUE_HEADS * HEAD_WIDTH), 1.0, 6.0, ((0, 4), (1, 4), (2, 2))),
        "source_len": with_ends(jax.random.randint(arg_keys[10], (MICRO_BATCHES,), SEQUENCE_TOKENS * 2 // 5, SEQUENCE_TOKENS * 9 // 10), jax.random.fold_in(arg_keys[10], 1), SEQUENCE_TOKENS * 2 // 5, (SEQUENCE_TOKENS * 9 // 10) - 1).astype(jnp.int32),
    }


precise = lax.Precision.HIGHEST

def mamba_one(mixer_in, gate_in, step_in, maps_in, decay_rate, skip_gain, norm_gain):
    x_heads = mixer_in.astype(jnp.float32).reshape(SEQUENCE_TOKENS, MH, HP)
    increment_collection = step_in.astype(jnp.float32)
    b_rows = maps_in[:, :NST].astype(jnp.float32)
    c_rows = maps_in[:, NST:].astype(jnp.float32)

    def advance(state, inputs):
        x_now, step_now, b_now, c_now = inputs
        state = jnp.exp(-decay_rate * step_now)[:, None, None] * state + step_now[:, None, None] * b_now[None, :, None] * x_now[:, None, :]
        present_result = jnp.einsum('n,hnp->hp', c_now, state, precision=precise) + skip_gain[:, None] * x_now
        return (state, present_result)
    start_state = jnp.zeros((MH, NST, HP), jnp.float32)
    _, outputs = lax.scan(advance, start_state, (x_heads, increment_collection, b_rows, c_rows))
    raw = outputs.reshape(SEQUENCE_TOKENS, EM).astype(jnp.bfloat16)
    gated = raw.astype(jnp.float32) * jax.nn.silu(gate_in.astype(jnp.float32))
    mean_sq = lax.optimization_barrier(jnp.mean(gated * gated, axis=-1))
    return (gated * lax.rsqrt(mean_sq + 1e-05)[:, None] * norm_gain[None, :]).astype(jnp.bfloat16)

def attention_one(query_matrix, key_matrix, content_array, source):
    group_width = QUERY_HEADS // KEY_VALUE_HEADS
    query_head_rows = query_matrix.astype(jnp.float32).reshape(SEQUENCE_TOKENS, KEY_VALUE_HEADS, group_width, HEAD_WIDTH).transpose(1, 0, 2, 3)
    key_head_rows = key_matrix.astype(jnp.float32).reshape(SEQUENCE_TOKENS, KEY_VALUE_HEADS, HEAD_WIDTH).transpose(1, 0, 2)
    value_head_rows = content_array.astype(jnp.float32).reshape(SEQUENCE_TOKENS, KEY_VALUE_HEADS, HEAD_WIDTH).transpose(1, 0, 2)
    rows_per = math.gcd(512, SEQUENCE_TOKENS)
    count = SEQUENCE_TOKENS // rows_per
    positions = jnp.arange(SEQUENCE_TOKENS, dtype=jnp.int32)
    scale = 1.0 / math.sqrt(HEAD_WIDTH)

    def per_head(operands):
        q_head, k_head, v_head = operands

        def per_block(block_idx):
            start = block_idx * rows_per
            q_block = lax.dynamic_slice_in_dim(q_head, start, rows_per, 0)
            scores = jnp.einsum('tgd,sd->gts', q_block, k_head, precision=precise) * scale
            query_pos = start + positions[:rows_per]
            visible = (positions[None, :] <= query_pos[:, None]) | (positions[None, :] < source)
            scores = jnp.where(visible[None], scores, -jnp.inf)
            top = lax.optimization_barrier(jnp.max(scores, axis=-1, keepdims=True))
            weights = jnp.exp(scores - top)
            totals = lax.optimization_barrier(jnp.sum(weights, axis=-1))
            rounded = weights.astype(jnp.bfloat16).astype(jnp.float32)
            mixed = jnp.einsum('gts,sd->tgd', rounded, v_head, precision=precise)
            return mixed / jnp.transpose(totals)[:, :, None]
        blocks_out = lax.map(per_block, jnp.arange(count, dtype=jnp.int32))
        return blocks_out.reshape(SEQUENCE_TOKENS, group_width, HEAD_WIDTH)
    heads_out = lax.map(per_head, (query_head_rows, key_head_rows, value_head_rows))
    return heads_out.transpose(1, 0, 2, 3).reshape(SEQUENCE_TOKENS, QUERY_HEADS * HEAD_WIDTH).astype(jnp.bfloat16)

def reference(mamba_input, mamba_gate, step_size, state_maps, decay_rate, skip_gain, norm_gain, queries, keys, values, source_len):
    mamba_list = []
    attention_list = []
    for member in range(MICRO_BATCHES):
        mamba_list.append(mamba_one(mamba_input[member], mamba_gate[member], step_size[member], state_maps[member], decay_rate, skip_gain, norm_gain))
        attention_list.append(attention_one(queries[member], keys[member], values[member], source_len[member]))
    mamba_all = jnp.stack(mamba_list, axis=0)
    attention_all = jnp.stack(attention_list, axis=0)
    return (jnp.roll(mamba_all, 1, axis=0), jnp.roll(attention_all, 1, axis=0))
```

```python
import functools
import math

import jax
import jax.numpy as jnp
from jax import lax
from jax.experimental import pallas as pl
from jax.experimental.pallas import tpu as pltpu
from jax.sharding import PartitionSpec as P

QUERY_HEADS = 64
KEY_VALUE_HEADS = 8
HEAD_WIDTH = 128
NST = 128
HP = 64
GROUP = QUERY_HEADS // KEY_VALUE_HEADS
CHUNKS = 4
VMEM = 40 * 1024 * 1024
HIGH = lax.Precision.HIGHEST


def dot(a, b, dims, precision=None):
    return lax.dot_general(
        a, b, (dims, ((), ())), precision=precision, preferred_element_type=jnp.float32
    )


def call(kernel, out_shape, flops, nbytes, **kw):
    return pl.pallas_call(
        kernel,
        out_shape=out_shape,
        compiler_params=pltpu.CompilerParams(vmem_limit_bytes=VMEM),
        cost_estimate=pl.CostEstimate(flops=flops, bytes_accessed=nbytes, transcendentals=0),
        **kw,
    )


def lower_mask(rows):
    return lax.broadcasted_iota(jnp.int32, (rows, rows), 0) >= lax.broadcasted_iota(
        jnp.int32, (rows, rows), 1
    )


def pair_columns(table, pair, rows):
    lane = lax.broadcasted_iota(jnp.int32, (rows, 2 * HP), 1)
    first = jnp.broadcast_to(table[:, 2 * pair : 2 * pair + 1], (rows, 2 * HP))
    second = jnp.broadcast_to(table[:, 2 * pair + 1 : 2 * pair + 2], (rows, 2 * HP))
    return jnp.where(lane < HP, first, second)


def state_kernel(x_ref, dt_ref, rate_ref, b_ref, state_ref, decay_ref, cum_ref, cum_t_ref, dt_t_ref):
    rows, heads = dt_ref.shape
    width = x_ref.shape[1] // CHUNKS
    lower = lower_mask(rows)
    ones = jnp.where(lower, 1.0, 0.0).astype(jnp.bfloat16)
    eye = jnp.where(
        lax.broadcasted_iota(jnp.int32, (rows, rows), 0)
        == lax.broadcasted_iota(jnp.int32, (rows, rows), 1),
        1.0,
        0.0,
    ).astype(jnp.bfloat16)
    dt = dt_ref[...]
    rate = rate_ref[...]
    cum = -rate * dot(ones, dt, ((1,), (0,)))
    cum_ref[...] = cum
    rate_col = jnp.transpose(jnp.broadcast_to(rate, (8, heads)))[:, :1]
    cum_t_ref[...] = -rate_col * dot(dt, ones, ((0,), (1,)))
    dt_t_ref[...] = dot(dt, eye, ((0,), (0,)))
    total = cum[rows - 1 : rows, :]
    tail = jnp.exp(total - cum) * dt.astype(jnp.float32)
    whole = jnp.exp(total)
    b = b_ref[...]
    for chunk in range(CHUNKS):
        for tile in range(width // 128):
            pair = chunk * (width // 128) + tile
            xs = x_ref[:, pair * 128 : pair * 128 + 128].astype(jnp.float32)
            xw = (xs * pair_columns(tail, pair, rows)).astype(jnp.bfloat16)
            state = dot(b, xw, ((0,), (0,)))
            state_ref[chunk, :, tile * 128 : tile * 128 + 128] = state.astype(state_ref.dtype)
            decay_ref[chunk, :, tile * 128 : tile * 128 + 128] = pair_columns(whole, pair, 1)


def inner_kernel(chunk, x_ref, skip_ref, maps_ref, cum_ref, cum_t_ref, dt_t_ref, out_ref):
    rows = x_ref.shape[0]
    width = x_ref.shape[1]
    gram = dot(maps_ref[:, NST:], maps_ref[:, :NST], ((1,), (1,)))
    gram = jnp.where(lower_mask(rows), gram, 0.0)
    lane = lax.broadcasted_iota(jnp.int32, (rows, 128), 1)
    cum = cum_ref[...]
    skip = skip_ref[...]
    for tile in range(width // 128):
        pair = chunk * (width // 128) + tile
        mixes = []
        for head in (2 * pair, 2 * pair + 1):
            mine = jnp.broadcast_to(cum[:, head : head + 1], (rows, rows))
            theirs = cum_t_ref[head : head + 1, :]
            decay = jnp.exp(jnp.minimum(mine - theirs, 0.0))
            mixes.append((gram * decay * dt_t_ref[head : head + 1, :]).astype(jnp.bfloat16))
        xs = x_ref[:, tile * 128 : tile * 128 + 128]
        zero = jnp.zeros_like(xs)
        stacked = jnp.concatenate(
            [jnp.where(lane < HP, xs, zero), jnp.where(lane < HP, zero, xs)], axis=0
        )
        mixed = dot(jnp.concatenate(mixes, axis=1), stacked, ((1,), (0,)))
        out_ref[:, tile * 128 : tile * 128 + 128] = mixed + pair_columns(
            skip, pair, 1
        ) * xs.astype(jnp.float32)


def gate_kernel(chunk, sources, index_ref, inner_ref, gate_ref, maps_ref, cum_ref, *refs):
    states, (out_ref, sums_ref, enter) = refs[:sources], refs[sources:]
    rows, width = out_ref.shape
    index = index_ref[0]

    @pl.when(index == 0)
    def _():
        enter[...] = jnp.zeros_like(enter)

    for source in range(sources):

        @pl.when(index == source + 1)
        def _(source=source):
            enter[...] = states[source][...].astype(jnp.bfloat16)

    grow = jnp.exp(cum_ref[...])
    outer = dot(maps_ref[:, NST:], enter[...], ((1,), (0,)))
    total = jnp.zeros((rows, 128), jnp.float32)
    for tile in range(width // 128):
        at = slice(tile * 128, tile * 128 + 128)
        pair = chunk * (width // 128) + tile
        raw = inner_ref[:, at] + pair_columns(grow, pair, rows) * outer[:, at]
        raw = raw.astype(jnp.bfloat16).astype(jnp.float32)
        gate = gate_ref[:, at].astype(jnp.float32)
        gated = raw * (gate / (1.0 + jnp.exp(-gate)))
        out_ref[:, at] = gated.astype(jnp.bfloat16)
        total = total + gated * gated
    sums_ref[...] = dot(jnp.ones((8, 128), jnp.float32), total, ((1,), (1,)), HIGH)


def norm_kernel(channels, *refs):
    *chunk_refs, sums_ref, gain_ref, out_ref = refs
    rows = out_ref.shape[0]
    mean = sums_ref[0:1, :] / channels
    scale = jnp.broadcast_to(lax.rsqrt(mean + 1e-05), (rows, rows))
    eye = lax.broadcasted_iota(jnp.int32, (rows, rows), 0) == lax.broadcasted_iota(
        jnp.int32, (rows, rows), 1
    )
    scale = jnp.sum(jnp.where(eye, scale, 0.0), axis=1, keepdims=True)
    at = 0
    for ref in chunk_refs:
        width = ref.shape[1]
        out_ref[:, at : at + width] = (
            ref[...].astype(jnp.float32) * scale * gain_ref[:, at : at + width]
        ).astype(jnp.bfloat16)
        at += width


def attention_kernel(ctx, index_ref, source_ref, q_ref, k_ref, v_ref, out_ref):
    rows = q_ref.shape[0]
    keys = k_ref.shape[0]
    index = index_ref[0]
    source = source_ref[0]
    lane = lax.broadcasted_iota(jnp.int32, (rows, keys), 1)
    owner = index - lane // rows
    owner = jnp.where(owner < 0, owner + ctx, owner)
    key_pos = owner * rows + lane % rows
    query_pos = index * rows + lax.broadcasted_iota(jnp.int32, (rows, keys), 0)
    visible = (key_pos <= query_pos) | (key_pos < source)
    factor = math.log2(math.e) / math.sqrt(HEAD_WIDTH)
    k = k_ref[...]
    v = v_ref[...]
    for head in range(GROUP):
        at = slice(head * HEAD_WIDTH, (head + 1) * HEAD_WIDTH)
        scores = dot(q_ref[:, at], k, ((1,), (1,))) * factor
        scores = jnp.where(visible, scores, -jnp.inf)
        top = jnp.max(scores, axis=1, keepdims=True)
        weights = jnp.exp2(scores - top)
        total = jnp.sum(weights, axis=1, keepdims=True)
        mixed = dot(weights.astype(jnp.bfloat16), v, ((1,), (0,)))
        out_ref[:, at] = (mixed / total).astype(jnp.bfloat16)


def on_device(
    mamba_input,
    mamba_gate,
    step_size,
    state_maps,
    decay_rate,
    skip_gain,
    norm_gain,
    queries,
    keys,
    values,
    source_len,
):
    segments = lax.axis_size("segment")
    ctx = lax.axis_size("ctx")
    tps = lax.axis_size("tp")
    index = lax.axis_index("ctx")
    index_in = index.astype(jnp.int32).reshape(1)
    onward = [(i, (i + 1) % segments) for i in range(segments)]

    def hand(array):
        return lax.ppermute(array, "segment", onward)

    x, gate, dt, maps = mamba_input[0], mamba_gate[0], step_size[0], state_maps[0]
    rows, channels = x.shape
    heads = dt.shape[1]
    width = channels // CHUNKS
    wire = jnp.bfloat16 if ctx <= 8 else jnp.float32
    f32 = jnp.float32

    source = hand(source_len)
    key_values = hand(jnp.concatenate([keys[0], values[0]], axis=1))
    query = hand(queries[0])

    rate = decay_rate.reshape(1, heads)
    skip = skip_gain.reshape(1, heads)
    shape = jax.ShapeDtypeStruct
    states, decays, cum, cum_t, dt_t = call(
        state_kernel,
        (
            shape((CHUNKS, NST, width), wire),
            shape((CHUNKS, 1, width), f32),
            shape((rows, heads), f32),
            shape((heads, rows), f32),
            shape((heads, rows), f32),
        ),
        2 * rows * NST * channels,
        4 * rows * channels,
    )(x, dt, rate, maps[:, :NST])

    chain = [(i, i + 1) for i in range(ctx - 1)]
    arrived = []
    for step in range(CHUNKS + ctx - 2):
        which = jnp.clip(step - index, 0, CHUNKS - 1)
        state = lax.dynamic_index_in_dim(states, which, 0, keepdims=False)
        if step > 0:
            decay = lax.dynamic_index_in_dim(decays, which, 0, keepdims=False)
            state = (arrived[-1].astype(f32) * decay + state.astype(f32)).astype(wire)
        arrived.append(lax.ppermute(state, "ctx", chain))

    pieces = [key_values]
    for distance in range(1, ctx):
        pieces.append(
            lax.ppermute(key_values, "ctx", [(i, (i + distance) % ctx) for i in range(ctx)])
        )
    all_key_values = jnp.concatenate(pieces, axis=0)
    all_rows = ctx * rows
    groups = keys.shape[2] // HEAD_WIDTH
    wide = GROUP * HEAD_WIDTH
    attention = call(
        functools.partial(attention_kernel, ctx),
        shape((rows, groups * wide), jnp.bfloat16),
        4 * rows * groups * wide * all_rows,
        4 * rows * groups * wide,
        grid=(groups,),
        in_specs=[
            pl.BlockSpec(memory_space=pltpu.SMEM),
            pl.BlockSpec(memory_space=pltpu.SMEM),
            pl.BlockSpec((rows, wide), lambda g: (0, g)),
            pl.BlockSpec((all_rows, HEAD_WIDTH), lambda g: (0, g)),
            pl.BlockSpec((all_rows, HEAD_WIDTH), lambda g: (0, g + groups)),
        ],
        out_specs=pl.BlockSpec((rows, wide), lambda g: (0, g)),
    )(index_in, source, query, all_key_values, all_key_values)

    handed = []
    sums = None
    whole = lambda *dims: pl.BlockSpec(dims, lambda i: (0,) * len(dims))
    for chunk in range(CHUNKS):
        block = pl.BlockSpec((rows, width), lambda i, chunk=chunk: (0, chunk))
        inner = call(
            functools.partial(inner_kernel, chunk),
            shape((rows, width), f32),
            2 * rows * rows * width,
            6 * rows * width,
            grid=(1,),
            in_specs=[block, whole(1, heads), whole(rows, 2 * NST), whole(rows, heads)]
            + [whole(heads, rows)] * 2,
            out_specs=whole(rows, width),
        )(x, skip, maps, cum, cum_t, dt_t)
        gated, part = call(
            functools.partial(gate_kernel, chunk, ctx - 1),
            (shape((rows, width), jnp.bfloat16), shape((8, rows), f32)),
            2 * rows * rows * width,
            8 * rows * width,
            grid=(1,),
            in_specs=[
                pl.BlockSpec(memory_space=pltpu.SMEM),
                whole(rows, width),
                block,
                whole(rows, 2 * NST),
                whole(rows, heads),
            ]
            + [whole(NST, width)] * (ctx - 1),
            out_specs=(whole(rows, width), whole(8, rows)),
            scratch_shapes=[pltpu.VMEM((NST, width), jnp.bfloat16)],
        )(index_in, inner, gate, maps, cum, *arrived[chunk : chunk + ctx - 1])
        handed.append(hand(gated))
        sums = part if sums is None else sums + part
    sums = hand(lax.psum(sums, "tp"))
    mamba = call(
        functools.partial(norm_kernel, channels * tps),
        shape((rows, channels), jnp.bfloat16),
        rows * channels,
        4 * rows * channels,
    )(*handed, sums, norm_gain.reshape(1, channels))
    return (mamba[None], attention[None])


def solution(mesh):
    placed = (
        P("segment", "ctx", "tp"),
        P("segment", "ctx", "tp"),
        P("segment", "ctx", "tp"),
        P("segment", "ctx", None),
        P("tp"),
        P("tp"),
        P("tp"),
        P("segment", "ctx", "tp"),
        P("segment", "ctx", "tp"),
        P("segment", "ctx", "tp"),
        P("segment"),
    )
    return jax.shard_map(
        on_device,
        mesh=mesh,
        in_specs=placed,
        out_specs=(P("segment", "ctx", "tp"), P("segment", "ctx", "tp")),
        check_vma=False,
    )
```

```python
import functools
import math

import jax
import jax.numpy as jnp
from jax import lax
from jax.experimental import pallas as pl
from jax.experimental.pallas import tpu as pltpu
from jax.sharding import PartitionSpec as P

QUERY_HEADS = 64
KEY_VALUE_HEADS = 8
HEAD_WIDTH = 128
NST = 128
HP = 64
GROUP = QUERY_HEADS // KEY_VALUE_HEADS
CHUNKS = 2
VMEM = 40 * 1024 * 1024
PARCEL_VMEM = 60 * 1024 * 1024
HIGH = lax.Precision.HIGHEST


def dot(a, b, dims, precision=None):
    return lax.dot_general(
        a, b, (dims, ((), ())), precision=precision, preferred_element_type=jnp.float32
    )


def call(kernel, out_shape, flops, nbytes, **kw):
    return pl.pallas_call(
        kernel,
        out_shape=out_shape,
        compiler_params=pltpu.CompilerParams(vmem_limit_bytes=VMEM),
        cost_estimate=pl.CostEstimate(flops=flops, bytes_accessed=nbytes, transcendentals=0),
        **kw,
    )


def lower_mask(rows):
    return lax.broadcasted_iota(jnp.int32, (rows, rows), 0) >= lax.broadcasted_iota(
        jnp.int32, (rows, rows), 1
    )


def pair_columns(table, pair, rows):
    lane = lax.broadcasted_iota(jnp.int32, (rows, 2 * HP), 1)
    first = jnp.broadcast_to(table[:, 2 * pair : 2 * pair + 1], (rows, 2 * HP))
    second = jnp.broadcast_to(table[:, 2 * pair + 1 : 2 * pair + 2], (rows, 2 * HP))
    return jnp.where(lane < HP, first, second)


def spread(row, first, width):
    return jnp.concatenate(
        [pair_columns(row, first // 2 + pair, 1) for pair in range(width // (2 * HP))], axis=1
    )


def parcel_kernel(index_ref, x_ref, maps_ref, dt_ref, key_ref, value_ref, *refs):
    *parcel_refs, packed_ref, sem = refs
    rows = x_ref.shape[0]
    side, half = x_ref.shape[1] // 2, dt_ref.shape[0] // 2
    width, kv = side // CHUNKS, key_ref.shape[1]
    away = 1 - index_ref[0] % 2
    first = parcel_refs[0]
    moves = [
        (
            x_ref.at[:, pl.ds(pl.multiple_of(away * side + chunk * width, 128), width)],
            out_ref.at[:, pl.ds(0, width)],
        )
        for chunk, out_ref in enumerate(parcel_refs)
    ]
    moves.append((maps_ref, first.at[:, pl.ds(width, 2 * NST)]))
    moves.append(
        (
            dt_ref.at[pl.ds(pl.multiple_of(away * half, half), half), :],
            first.at[pl.ds(0, half), pl.ds(width + 2 * NST, rows)],
        )
    )
    moves.append((key_ref, packed_ref.at[:, pl.ds(0, kv)]))
    moves.append((value_ref, packed_ref.at[:, pl.ds(kv, kv)]))
    copies = [
        pltpu.make_async_copy(src, dst, sem.at[number]) for number, (src, dst) in enumerate(moves)
    ]
    for copy in copies:
        copy.start()
    for copy in copies:
        copy.wait()


def decays(dt, rate, heads):
    rows = dt.shape[1]
    ones = jnp.where(lower_mask(rows), 1.0, 0.0).astype(jnp.bfloat16)
    rate_col = jnp.transpose(jnp.broadcast_to(rate, (8, heads)))[:, :1]
    cum = -rate * dot(ones, dt, ((1,), (1,)))
    cum_t = -rate_col * dot(dt, ones, ((1,), (1,)))
    return cum, cum_t


def state_kernel(
    chunk, index_ref, x_ref, x2_ref, dt_ref, dt2_ref, rate_ref, b_ref, b2_ref,
    out_ref, first_ref, lead_ref, both_ref,
):
    rows, width = x_ref.shape
    count = width // HP
    at = slice(chunk * count, chunk * count + count)
    early = index_ref[0] % 2 == 0
    rate = rate_ref[0][:, at]
    halves = []
    for x, dt, b in ((x_ref, dt_ref, b_ref), (x2_ref, dt2_ref, b2_ref)):
        step = dt[at, :]
        cum, _ = decays(step, rate, count)
        total = cum[rows - 1 : rows, :]
        tail = jnp.exp(total - cum) * jnp.transpose(step.astype(jnp.float32))
        xw = jnp.concatenate(
            [
                (
                    x[:, pair * 128 : pair * 128 + 128].astype(jnp.float32)
                    * pair_columns(tail, pair, rows)
                ).astype(jnp.bfloat16)
                for pair in range(width // 128)
            ],
            axis=1,
        )
        halves.append((dot(b[...], xw, ((0,), (0,))), spread(jnp.exp(total), 0, width)))
    (mine, mine_decay), (theirs, theirs_decay) = halves
    first = jnp.where(early, mine, theirs)
    second = jnp.where(early, theirs, mine)
    lead = jnp.where(early, mine_decay, theirs_decay)
    trail = jnp.where(early, theirs_decay, mine_decay)
    out_ref[...] = (first * trail + second).astype(out_ref.dtype)
    first_ref[...] = first
    lead_ref[...] = lead
    both_ref[...] = lead * trail


def inner_kernel(
    chunk, index_ref, x_ref, x2_ref, dt_ref, dt2_ref, rate_ref, skip_ref, maps_ref, maps2_ref,
    out_ref, grow_ref, out2_ref, grow2_ref,
):
    del index_ref
    rows, width = x_ref.shape
    count = width // HP
    at = slice(chunk * count, chunk * count + count)
    lane = lax.broadcasted_iota(jnp.int32, (rows, 128), 1)
    rate, skip = rate_ref[0][:, at], skip_ref[0][:, at]
    for x, dt, maps, out, spread_out in (
        (x_ref, dt_ref, maps_ref, out_ref, grow_ref),
        (x2_ref, dt2_ref, maps2_ref, out2_ref, grow2_ref),
    ):
        gram = dot(maps[:, NST:], maps[:, :NST], ((1,), (1,)))
        gram = jnp.where(lower_mask(rows), gram, 0.0)
        step = dt[at, :]
        cum, cum_t = decays(step, rate, count)
        step = step.astype(jnp.float32)
        grow = jnp.exp(cum)
        for pair in range(width // 128):
            mixes = []
            for head in (2 * pair, 2 * pair + 1):
                mine = jnp.broadcast_to(cum[:, head : head + 1], (rows, rows))
                decay = jnp.exp(jnp.minimum(mine - cum_t[head : head + 1, :], 0.0))
                mixes.append((gram * decay * step[head : head + 1, :]).astype(jnp.bfloat16))
            xs = x[:, pair * 128 : pair * 128 + 128]
            zero = jnp.zeros_like(xs)
            stacked = jnp.concatenate(
                [jnp.where(lane < HP, xs, zero), jnp.where(lane < HP, zero, xs)], axis=0
            )
            mixed = dot(jnp.concatenate(mixes, axis=1), stacked, ((1,), (0,)))
            mixed = mixed + pair_columns(skip, pair, 1) * xs.astype(jnp.float32)
            out[:, pair * 128 : pair * 128 + 128] = mixed
            spread_out[:, pair * 128 : pair * 128 + 128] = pair_columns(grow, pair, rows)


def gate_and_sum(raw, gate, out_ref, sums_ref):
    rows, width = raw.shape
    gate = gate.astype(jnp.float32)
    gated = raw.astype(jnp.float32) * (gate / (1.0 + jnp.exp(-gate)))
    out_ref[...] = gated.astype(jnp.bfloat16)
    squares = gated * gated
    total = squares[:, :128]
    for tile in range(1, width // 128):
        total = total + squares[:, tile * 128 : tile * 128 + 128]
    sums_ref[...] = dot(jnp.ones((8, 128), jnp.float32), total, ((1,), (1,)), HIGH)


def outer_kernel(
    index_ref, enter_ref, first_ref, lead_ref, local_ref, grow_ref, local2_ref, grow2_ref,
    c_ref, c2_ref, gate_ref, out_ref, sums_ref, back_ref,
):
    early = index_ref[0] % 2 == 0
    enter = jnp.where(index_ref[0] < 2, 0.0, enter_ref[...].astype(jnp.float32))
    later = lead_ref[...] * enter + first_ref[...]
    mine = jnp.where(early, enter, later).astype(jnp.bfloat16)
    theirs = jnp.where(early, later, enter).astype(jnp.bfloat16)
    back = local2_ref[...] + grow2_ref[...] * dot(c2_ref[...], theirs, ((1,), (0,)))
    back_ref[...] = back.astype(jnp.bfloat16)
    raw = local_ref[...] + grow_ref[...] * dot(c_ref[...], mine, ((1,), (0,)))
    gate_and_sum(raw.astype(jnp.bfloat16), gate_ref[...], out_ref, sums_ref)


def gate_kernel(index_ref, raw_ref, gate_ref, out_ref, sums_ref):
    del index_ref
    gate_and_sum(raw_ref[...], gate_ref[...], out_ref, sums_ref)


def norm_kernel(channels, index_ref, *refs):
    *chunk_refs, sums_ref, gain_ref, out_ref = refs
    rows = out_ref.shape[0]
    half = out_ref.shape[1] // 2
    mean = sums_ref[0:1, :] / channels
    scale = jnp.broadcast_to(lax.rsqrt(mean + 1e-05), (rows, rows))
    eye = lax.broadcasted_iota(jnp.int32, (rows, rows), 0) == lax.broadcasted_iota(
        jnp.int32, (rows, rows), 1
    )
    scale = jnp.sum(jnp.where(eye, scale, 0.0), axis=1, keepdims=True)
    parity = index_ref[0] % 2
    for number, ref in enumerate(chunk_refs):
        width = ref.shape[1]
        side, chunk = divmod(number, CHUNKS)
        start = (parity if side == 0 else 1 - parity) * half + chunk * width
        at = pl.ds(pl.multiple_of(start, 128), width)
        out_ref[:, at] = (ref[...].astype(jnp.float32) * scale * gain_ref[:, at]).astype(
            jnp.bfloat16
        )


def attention_kernel(ctx, index_ref, source_ref, q_ref, *refs):
    out_ref, bias_ref = refs[-2:]
    key = jnp.concatenate([ref[...] for ref in refs[:ctx]], axis=0)
    value = jnp.concatenate([ref[...] for ref in refs[ctx : 2 * ctx]], axis=0)
    rows = q_ref.shape[0]
    keys = key.shape[0]
    index = index_ref[0]
    source = source_ref[0]
    place = lax.broadcasted_iota(jnp.int32, (keys, rows), 0)
    away = place // rows
    owner = jnp.zeros_like(place)
    step, bit = ctx // 2, 1
    while step >= 1:
        owner = owner + jnp.where((away & bit) != 0, step, 0)
        step, bit = step // 2, bit * 2
    key_pos = (owner ^ index) * rows + place % rows
    query_pos = index * rows + lax.broadcasted_iota(jnp.int32, (keys, rows), 1)
    bias_ref[...] = jnp.where((key_pos <= query_pos) | (key_pos < source), 0.0, -jnp.inf)
    factor = math.log2(math.e) / math.sqrt(HEAD_WIDTH)
    span = lambda head: slice(head * HEAD_WIDTH, (head + 1) * HEAD_WIDTH)
    query = jnp.concatenate([q_ref[:, span(head)] for head in range(GROUP)], axis=0)
    value = jnp.transpose(value.astype(jnp.float32)).astype(jnp.bfloat16)
    scores = dot(key, query, ((1,), (1,)))
    weights, totals = [], []
    for head in range(GROUP):
        kept = scores[:, head * rows : (head + 1) * rows] + bias_ref[...]
        top = jnp.max(kept, axis=0, keepdims=True)
        weight = jnp.exp2((kept - top) * factor)
        totals.append(jnp.sum(weight, axis=0, keepdims=True))
        weights.append(weight.astype(jnp.bfloat16))
    mixed = dot(value, jnp.concatenate(weights, axis=1), ((1,), (0,)))
    mixed = mixed / jnp.concatenate(totals, axis=1)
    for head in range(GROUP):
        out_ref[:, span(head)] = jnp.transpose(
            mixed[:, head * rows : (head + 1) * rows]
        ).astype(jnp.bfloat16)


def on_device(
    mamba_input,
    mamba_gate,
    step_size,
    state_maps,
    decay_rate,
    skip_gain,
    norm_gain,
    queries,
    keys,
    values,
    source_len,
):
    segments = lax.axis_size("segment")
    ctx = lax.axis_size("ctx")
    tps = lax.axis_size("tp")
    index = lax.axis_index("ctx")
    index_in = index.astype(jnp.int32).reshape(1)
    onward = [(i, (i + 1) % segments) for i in range(segments)]
    partner = [(i, i + 1 - 2 * (i % 2)) for i in range(ctx)]
    further = [(i, (i + 2) % ctx) for i in range(ctx)]
    bf16, f32 = jnp.bfloat16, jnp.float32
    shape = jax.ShapeDtypeStruct

    def hand(array):
        return lax.ppermute(array, "segment", onward)

    def after(value, *others):
        return lax.optimization_barrier((value, *others))[0]

    x, gate, maps = mamba_input[0], mamba_gate[0], state_maps[0]
    dt = step_size[0].T
    heads, rows = dt.shape
    channels = x.shape[1]
    half = heads // 2
    side = channels // 2
    width = side // CHUNKS
    wire = bf16 if ctx <= 8 else f32
    rate = decay_rate.reshape(2, 1, half)
    skip = skip_gain.reshape(2, 1, half)
    groups = keys.shape[2] // HEAD_WIDTH
    wide = GROUP * HEAD_WIDTH

    whole = lambda *dims: pl.BlockSpec(dims, lambda i, s: (0,) * len(dims))
    fixed = lambda dims, *at: pl.BlockSpec(dims, lambda i, s: at)
    mine = lambda dims: pl.BlockSpec(dims, lambda i, s: (s[0] % 2,) + (0,) * (len(dims) - 1))
    columns = lambda chunk: pl.BlockSpec(
        (rows, width), lambda i, s: (0, (s[0] % 2) * CHUNKS + chunk)
    )
    others = lambda chunk: pl.BlockSpec(
        (rows, width), lambda i, s: (0, (1 - s[0] % 2) * CHUNKS + chunk)
    )

    def indexed(kernel, out_shape, flops, nbytes, in_specs, out_specs, scratch=(), vmem=VMEM):
        return pl.pallas_call(
            kernel,
            out_shape=out_shape,
            grid_spec=pltpu.PrefetchScalarGridSpec(
                num_scalar_prefetch=1,
                grid=(1,),
                in_specs=in_specs,
                out_specs=out_specs,
                scratch_shapes=scratch,
            ),
            compiler_params=pltpu.CompilerParams(vmem_limit_bytes=vmem),
            cost_estimate=pl.CostEstimate(flops=flops, bytes_accessed=nbytes, transcendentals=0),
        )

    parcel_width = width + 2 * NST + rows
    hbm = pl.BlockSpec(memory_space=pltpu.HBM)
    kv_width = 2 * groups * HEAD_WIDTH
    *parcels, packed = indexed(
        parcel_kernel,
        (shape((rows, parcel_width), bf16),)
        + (shape((rows, width), bf16),) * (CHUNKS - 1)
        + (shape((rows, kv_width), bf16),),
        0,
        4 * rows * side,
        [hbm] * 5,
        (whole(rows, parcel_width),)
        + (whole(rows, width),) * (CHUNKS - 1)
        + (whole(rows, kv_width),),
        [pltpu.SemaphoreType.DMA((CHUNKS + 4,))],
        PARCEL_VMEM,
    )(index_in, x, maps, dt, keys[0], values[0])
    got = [lax.ppermute(parcel, "ctx", partner) for parcel in parcels]
    key_values = hand(packed)
    query = hand(queries[0])
    source = hand(source_len)
    pairs = [
        columns,
        lambda chunk: whole(rows, width),
        lambda chunk: mine((half, rows)),
        lambda chunk: fixed((half, rows), 0, (width + 2 * NST) // rows),
        lambda chunk: mine((1, 1, half)),
    ]
    places = lambda chunk: [spec(chunk) for spec in pairs]
    states, firsts, leads, inner = [], [], [], []
    for chunk in range(CHUNKS):
        state, first, lead, both = indexed(
            functools.partial(state_kernel, chunk),
            (shape((NST, width), wire), shape((NST, width), f32)) + (shape((1, width), f32),) * 2,
            4 * rows * NST * width,
            4 * rows * width,
            places(chunk) + [whole(rows, NST), fixed((rows, NST), 0, width // NST)],
            (whole(NST, width),) * 2 + (whole(1, width),) * 2,
        )(index_in, x, got[chunk], dt, got[0], rate, maps, got[0])
        enter = lax.ppermute(state, "ctx", further)
        for _ in range(ctx // 2 - 2):
            enter = jnp.where(index < 2, 0.0, enter.astype(f32))
            enter = lax.ppermute((state.astype(f32) + both * enter).astype(wire), "ctx", further)
        states.append(enter)
        firsts.append(first)
        leads.append(lead)
    for chunk in range(CHUNKS):
        inner.append(
            indexed(
                functools.partial(inner_kernel, chunk),
                (shape((rows, width), f32),) * 4,
                8 * rows * rows * width,
                6 * rows * width,
                places(chunk)
                + [
                    mine((1, 1, half)),
                    whole(rows, 2 * NST),
                    fixed((rows, 2 * NST), 0, width // (2 * NST)),
                ],
                (whole(rows, width),) * 4,
            )(index_in, x, got[chunk], dt, got[0], rate, skip, maps, got[0])
        )
    scalar = pl.BlockSpec(memory_space=pltpu.SMEM)

    def attend(group, query, pieces, out):
        more = [] if out is None else [out]
        spot = lambda at: pl.BlockSpec((rows, HEAD_WIDTH), lambda i: (0, at))
        return call(
            functools.partial(attention_kernel, ctx),
            shape((rows, groups * wide), bf16),
            4 * rows * wide * ctx * rows,
            4 * rows * wide,
            grid=(1,),
            in_specs=[scalar, scalar, pl.BlockSpec((rows, wide), lambda i: (0, group))]
            + [spot(group)] * ctx
            + [spot(group + groups)] * ctx
            + [pl.BlockSpec(memory_space=pl.ANY)] * len(more),
            out_specs=pl.BlockSpec((rows, wide), lambda i: (0, group)),
            scratch_shapes=[pltpu.VMEM((ctx * rows, rows), f32)],
            input_output_aliases={3 + 2 * ctx: 0} if more else {},
        )(index_in, source, query, *pieces, *pieces, *more)

    pieces = [after(key_values, states[0])]
    step = ctx // 2
    while step >= 1:
        swap = [(i, i ^ step) for i in range(ctx)]
        pieces = pieces + [lax.ppermute(piece, "ctx", swap) for piece in pieces]
        step //= 2

    gated, sums, back = [], [], []
    for chunk in range(CHUNKS):
        some, part, away = indexed(
            outer_kernel,
            (shape((rows, width), bf16), shape((8, rows), f32), shape((rows, width), bf16)),
            4 * rows * rows * width,
            8 * rows * width,
            [whole(NST, width)] * 2
            + [whole(1, width)]
            + [whole(rows, width)] * 4
            + [
                fixed((rows, NST), 0, 1),
                fixed((rows, NST), 0, width // NST + 1),
                columns(chunk),
            ],
            (whole(rows, width), whole(8, rows), whole(rows, width)),
        )(index_in, states[chunk], firsts[chunk], leads[chunk], *inner[chunk], maps, got[0], gate)
        gated.append(hand(some))
        sums.append(part)
        back.append(lax.ppermute(away, "ctx", partner))
    for chunk in range(CHUNKS):
        some, part = indexed(
            gate_kernel,
            (shape((rows, width), bf16), shape((8, rows), f32)),
            2 * rows * width,
            8 * rows * width,
            [whole(rows, width), others(chunk)],
            (whole(rows, width), whole(8, rows)),
        )(index_in, after(back[chunk], query, source, gated[chunk]), gate)
        gated.append(hand(some))
        sums.append(part)
    attention = None
    for group in range(groups):
        attention = attend(group, after(query, some, *gated[:3]), pieces, attention)
    sums = sum(sums)
    swap = [(i, (i + step) % tps) for step in range(1, tps) for i in range(tps)]
    sums = hand(sums + lax.ppermute(sums, "tp", swap))

    mamba = indexed(
        functools.partial(norm_kernel, channels * tps),
        shape((rows, channels), bf16),
        rows * channels,
        4 * rows * channels,
        [whole(rows, width)] * (2 * CHUNKS) + [whole(8, rows), whole(1, channels)],
        whole(rows, channels),
    )(index_in, *gated, sums, norm_gain.reshape(1, channels))
    return (mamba[None], attention[None])


def solution(mesh):
    placed = (
        P("segment", "ctx", "tp"),
        P("segment", "ctx", "tp"),
        P("segment", "ctx", "tp"),
        P("segment", "ctx", None),
        P("tp"),
        P("tp"),
        P("tp"),
        P("segment", "ctx", "tp"),
        P("segment", "ctx", "tp"),
        P("segment", "ctx", "tp"),
        P("segment"),
    )
    return jax.shard_map(
        on_device,
        mesh=mesh,
        in_specs=placed,
        out_specs=(P("segment", "ctx", "tp"), P("segment", "ctx", "tp")),
        check_vma=False,
    )
```

```python
import functools
import math

import jax
import jax.numpy as jnp
from jax import lax
from jax.experimental import pallas as pl
from jax.experimental.pallas import tpu as pltpu
from jax.sharding import PartitionSpec as P

QUERY_HEADS = 64
KEY_VALUE_HEADS = 8
HEAD_WIDTH = 128
NST = 128
HP = 64
GROUP = QUERY_HEADS // KEY_VALUE_HEADS
CHUNKS = 2
VMEM = 40 * 1024 * 1024
PARCEL_VMEM = 60 * 1024 * 1024
HIGH = lax.Precision.HIGHEST


def dot(a, b, dims, precision=None):
    return lax.dot_general(
        a, b, (dims, ((), ())), precision=precision, preferred_element_type=jnp.float32
    )


def call(kernel, out_shape, flops, nbytes, **kw):
    return pl.pallas_call(
        kernel,
        out_shape=out_shape,
        compiler_params=pltpu.CompilerParams(vmem_limit_bytes=VMEM),
        cost_estimate=pl.CostEstimate(flops=flops, bytes_accessed=nbytes, transcendentals=0),
        **kw,
    )


def lower_mask(rows):
    return lax.broadcasted_iota(jnp.int32, (rows, rows), 0) >= lax.broadcasted_iota(
        jnp.int32, (rows, rows), 1
    )


def pair_columns(table, pair, rows):
    lane = lax.broadcasted_iota(jnp.int32, (rows, 2 * HP), 1)
    first = jnp.broadcast_to(table[:, 2 * pair : 2 * pair + 1], (rows, 2 * HP))
    second = jnp.broadcast_to(table[:, 2 * pair + 1 : 2 * pair + 2], (rows, 2 * HP))
    return jnp.where(lane < HP, first, second)


def spread(row, first, width):
    return jnp.concatenate(
        [pair_columns(row, first // 2 + pair, 1) for pair in range(width // (2 * HP))], axis=1
    )


def parcel_kernel(
    index_ref, x_ref, maps_ref, dt_ref, key_ref, value_ref, rate_ref, skip_ref, *refs
):
    *parcel_refs, packed_ref, rate_out, skip_out, sem = refs
    rows = x_ref.shape[0]
    side, half = x_ref.shape[1] // 2, dt_ref.shape[0] // 2
    width, kv = side // CHUNKS, key_ref.shape[1]
    away = 1 - index_ref[0] % 2
    first = parcel_refs[0]
    moves = [
        (
            x_ref.at[:, pl.ds(pl.multiple_of(away * side + chunk * width, 128), width)],
            out_ref.at[:, pl.ds(0, width)],
        )
        for chunk, out_ref in enumerate(parcel_refs)
    ]
    moves.append((maps_ref, first.at[:, pl.ds(width, 2 * NST)]))
    moves.append(
        (
            dt_ref.at[pl.ds(pl.multiple_of(away * half, half), half), :],
            first.at[pl.ds(0, half), pl.ds(width + 2 * NST, rows)],
        )
    )
    moves.append((key_ref, packed_ref.at[:, pl.ds(0, kv)]))
    moves.append((value_ref, packed_ref.at[:, pl.ds(kv, kv)]))
    moves.append((rate_ref, rate_out))
    moves.append((skip_ref, skip_out))
    copies = [
        pltpu.make_async_copy(src, dst, sem.at[number]) for number, (src, dst) in enumerate(moves)
    ]
    for copy in copies:
        copy.start()
    for copy in copies:
        copy.wait()


def own_heads(ref, early, chunk, count):
    row = ref[...]
    half = row.shape[1] // 2
    low = row[:, chunk * count : chunk * count + count]
    high = row[:, half + chunk * count : half + chunk * count + count]
    return jnp.where(early, low, high)


def decays(dt, rate, heads):
    rows = dt.shape[1]
    ones = jnp.where(lower_mask(rows), 1.0, 0.0).astype(jnp.bfloat16)
    rate_col = jnp.transpose(jnp.broadcast_to(rate, (8, heads)))[:, :1]
    cum = -rate * dot(ones, dt, ((1,), (1,)))
    cum_t = -rate_col * dot(dt, ones, ((1,), (1,)))
    return cum, cum_t


def state_kernel(
    chunk, index_ref, x_ref, x2_ref, dt_ref, dt2_ref, rate_ref, b_ref, b2_ref,
    out_ref, first_ref, lead_ref, both_ref,
):
    rows, width = x_ref.shape
    count = width // HP
    at = slice(chunk * count, chunk * count + count)
    early = index_ref[0] % 2 == 0
    rate = own_heads(rate_ref, early, chunk, count)
    halves = []
    for x, dt, b in ((x_ref, dt_ref, b_ref), (x2_ref, dt2_ref, b2_ref)):
        step = dt[at, :]
        cum, _ = decays(step, rate, count)
        total = cum[rows - 1 : rows, :]
        tail = jnp.exp(total - cum) * jnp.transpose(step.astype(jnp.float32))
        xw = jnp.concatenate(
            [
                (
                    x[:, pair * 128 : pair * 128 + 128].astype(jnp.float32)
                    * pair_columns(tail, pair, rows)
                ).astype(jnp.bfloat16)
                for pair in range(width // 128)
            ],
            axis=1,
        )
        halves.append((dot(b[...], xw, ((0,), (0,))), spread(jnp.exp(total), 0, width)))
    (mine, mine_decay), (theirs, theirs_decay) = halves
    first = jnp.where(early, mine, theirs)
    second = jnp.where(early, theirs, mine)
    lead = jnp.where(early, mine_decay, theirs_decay)
    trail = jnp.where(early, theirs_decay, mine_decay)
    out_ref[...] = (first * trail + second).astype(out_ref.dtype)
    first_ref[...] = first
    lead_ref[...] = lead
    both_ref[...] = lead * trail


def inner_kernel(
    chunk, index_ref, x_ref, x2_ref, dt_ref, dt2_ref, rate_ref, skip_ref, maps_ref, maps2_ref,
    out_ref, grow_ref, out2_ref, grow2_ref,
):
    early = index_ref[0] % 2 == 0
    rows, width = x_ref.shape
    count = width // HP
    at = slice(chunk * count, chunk * count + count)
    lane = lax.broadcasted_iota(jnp.int32, (rows, 128), 1)
    rate = own_heads(rate_ref, early, chunk, count)
    skip = own_heads(skip_ref, early, chunk, count)
    for x, dt, maps, out, spread_out in (
        (x_ref, dt_ref, maps_ref, out_ref, grow_ref),
        (x2_ref, dt2_ref, maps2_ref, out2_ref, grow2_ref),
    ):
        gram = dot(maps[:, NST:], maps[:, :NST], ((1,), (1,)))
        gram = jnp.where(lower_mask(rows), gram, 0.0)
        step = dt[at, :]
        cum, cum_t = decays(step, rate, count)
        step = step.astype(jnp.float32)
        grow = jnp.exp(cum)
        for pair in range(width // 128):
            mixes = []
            for head in (2 * pair, 2 * pair + 1):
                mine = jnp.broadcast_to(cum[:, head : head + 1], (rows, rows))
                decay = jnp.exp(jnp.minimum(mine - cum_t[head : head + 1, :], 0.0))
                mixes.append((gram * decay * step[head : head + 1, :]).astype(jnp.bfloat16))
            xs = x[:, pair * 128 : pair * 128 + 128]
            zero = jnp.zeros_like(xs)
            stacked = jnp.concatenate(
                [jnp.where(lane < HP, xs, zero), jnp.where(lane < HP, zero, xs)], axis=0
            )
            mixed = dot(jnp.concatenate(mixes, axis=1), stacked, ((1,), (0,)))
            mixed = mixed + pair_columns(skip, pair, 1) * xs.astype(jnp.float32)
            out[:, pair * 128 : pair * 128 + 128] = mixed
            spread_out[:, pair * 128 : pair * 128 + 128] = pair_columns(grow, pair, rows)


def gate_and_sum(raw, gate, out_ref, sums_ref):
    rows, width = raw.shape
    gate = gate.astype(jnp.float32)
    gated = raw.astype(jnp.float32) * (gate / (1.0 + jnp.exp(-gate)))
    out_ref[...] = gated.astype(jnp.bfloat16)
    squares = gated * gated
    total = squares[:, :128]
    for tile in range(1, width // 128):
        total = total + squares[:, tile * 128 : tile * 128 + 128]
    sums_ref[...] = dot(jnp.ones((8, 128), jnp.float32), total, ((1,), (1,)), HIGH)


def outer_kernel(
    index_ref, enter_ref, first_ref, lead_ref, local_ref, grow_ref, local2_ref, grow2_ref,
    c_ref, c2_ref, gate_ref, out_ref, sums_ref, back_ref,
):
    early = index_ref[0] % 2 == 0
    enter = jnp.where(index_ref[0] < 2, 0.0, enter_ref[...].astype(jnp.float32))
    later = lead_ref[...] * enter + first_ref[...]
    mine = jnp.where(early, enter, later).astype(jnp.bfloat16)
    theirs = jnp.where(early, later, enter).astype(jnp.bfloat16)
    back = local2_ref[...] + grow2_ref[...] * dot(c2_ref[...], theirs, ((1,), (0,)))
    back_ref[...] = back.astype(jnp.bfloat16)
    raw = local_ref[...] + grow_ref[...] * dot(c_ref[...], mine, ((1,), (0,)))
    gate_and_sum(raw.astype(jnp.bfloat16), gate_ref[...], out_ref, sums_ref)


def gate_kernel(index_ref, raw_ref, gate_ref, out_ref, sums_ref):
    del index_ref
    gate_and_sum(raw_ref[...], gate_ref[...], out_ref, sums_ref)


def norm_kernel(channels, index_ref, *refs):
    *chunk_refs, sums_ref, gain_ref, out_ref = refs
    rows = out_ref.shape[0]
    half = out_ref.shape[1] // 2
    mean = sums_ref[0:1, :] / channels
    scale = jnp.broadcast_to(lax.rsqrt(mean + 1e-05), (rows, rows))
    eye = lax.broadcasted_iota(jnp.int32, (rows, rows), 0) == lax.broadcasted_iota(
        jnp.int32, (rows, rows), 1
    )
    scale = jnp.sum(jnp.where(eye, scale, 0.0), axis=1, keepdims=True)
    parity = index_ref[0] % 2
    for number, ref in enumerate(chunk_refs):
        width = ref.shape[1]
        side, chunk = divmod(number, CHUNKS)
        start = (parity if side == 0 else 1 - parity) * half + chunk * width
        at = pl.ds(pl.multiple_of(start, 128), width)
        out_ref[:, at] = (ref[...].astype(jnp.float32) * scale * gain_ref[:, at]).astype(
            jnp.bfloat16
        )


def attention_kernel(ctx, index_ref, source_ref, q_ref, *refs):
    out_ref, bias_ref = refs[-2:]
    key = jnp.concatenate([ref[...] for ref in refs[:ctx]], axis=0)
    value = jnp.concatenate([ref[...] for ref in refs[ctx : 2 * ctx]], axis=0)
    rows = q_ref.shape[0]
    keys = key.shape[0]
    index = index_ref[0]
    source = source_ref[0]
    place = lax.broadcasted_iota(jnp.int32, (keys, rows), 0)
    away = place // rows
    owner = jnp.zeros_like(place)
    step, bit = ctx // 2, 1
    while step >= 1:
        owner = owner + jnp.where((away & bit) != 0, step, 0)
        step, bit = step // 2, bit * 2
    key_pos = (owner ^ index) * rows + place % rows
    query_pos = index * rows + lax.broadcasted_iota(jnp.int32, (keys, rows), 1)
    bias_ref[...] = jnp.where((key_pos <= query_pos) | (key_pos < source), 0.0, -jnp.inf)
    factor = math.log2(math.e) / math.sqrt(HEAD_WIDTH)
    span = lambda head: slice(head * HEAD_WIDTH, (head + 1) * HEAD_WIDTH)
    query = jnp.concatenate([q_ref[:, span(head)] for head in range(GROUP)], axis=0)
    value = jnp.transpose(value.astype(jnp.float32)).astype(jnp.bfloat16)
    scores = dot(key, query, ((1,), (1,)))
    weights, totals = [], []
    for head in range(GROUP):
        kept = scores[:, head * rows : (head + 1) * rows] + bias_ref[...]
        top = jnp.max(kept, axis=0, keepdims=True)
        weight = jnp.exp2((kept - top) * factor)
        totals.append(jnp.sum(weight, axis=0, keepdims=True))
        weights.append(weight.astype(jnp.bfloat16))
    mixed = dot(value, jnp.concatenate(weights, axis=1), ((1,), (0,)))
    mixed = mixed / jnp.concatenate(totals, axis=1)
    for head in range(GROUP):
        out_ref[:, span(head)] = jnp.transpose(
            mixed[:, head * rows : (head + 1) * rows]
        ).astype(jnp.bfloat16)


def on_device(
    mamba_input,
    mamba_gate,
    step_size,
    state_maps,
    decay_rate,
    skip_gain,
    norm_gain,
    queries,
    keys,
    values,
    source_len,
):
    segments = lax.axis_size("segment")
    ctx = lax.axis_size("ctx")
    tps = lax.axis_size("tp")
    index = lax.axis_index("ctx")
    index_in = index.astype(jnp.int32).reshape(1)
    onward = [(i, (i + 1) % segments) for i in range(segments)]
    partner = [(i, i + 1 - 2 * (i % 2)) for i in range(ctx)]
    further = [(i, (i + 2) % ctx) for i in range(ctx)]
    bf16, f32 = jnp.bfloat16, jnp.float32
    shape = jax.ShapeDtypeStruct

    def hand(array):
        return lax.ppermute(array, "segment", onward)

    def after(value, *others):
        return lax.optimization_barrier((value, *others))[0]

    x, gate, maps = mamba_input[0], mamba_gate[0], state_maps[0]
    dt = step_size[0].T
    heads, rows = dt.shape
    channels = x.shape[1]
    half = heads // 2
    side = channels // 2
    width = side // CHUNKS
    wire = bf16 if ctx <= 8 else f32
    groups = keys.shape[2] // HEAD_WIDTH
    wide = GROUP * HEAD_WIDTH

    whole = lambda *dims: pl.BlockSpec(dims, lambda i, s: (0,) * len(dims))
    fixed = lambda dims, *at: pl.BlockSpec(dims, lambda i, s: at)
    mine = lambda dims: pl.BlockSpec(dims, lambda i, s: (s[0] % 2,) + (0,) * (len(dims) - 1))
    columns = lambda chunk: pl.BlockSpec(
        (rows, width), lambda i, s: (0, (s[0] % 2) * CHUNKS + chunk)
    )
    others = lambda chunk: pl.BlockSpec(
        (rows, width), lambda i, s: (0, (1 - s[0] % 2) * CHUNKS + chunk)
    )

    def indexed(kernel, out_shape, flops, nbytes, in_specs, out_specs, scratch=(), vmem=VMEM):
        return pl.pallas_call(
            kernel,
            out_shape=out_shape,
            grid_spec=pltpu.PrefetchScalarGridSpec(
                num_scalar_prefetch=1,
                grid=(1,),
                in_specs=in_specs,
                out_specs=out_specs,
                scratch_shapes=scratch,
            ),
            compiler_params=pltpu.CompilerParams(vmem_limit_bytes=vmem),
            cost_estimate=pl.CostEstimate(flops=flops, bytes_accessed=nbytes, transcendentals=0),
        )

    parcel_width = width + 2 * NST + rows
    hbm = pl.BlockSpec(memory_space=pltpu.HBM)
    kv_width = 2 * groups * HEAD_WIDTH
    *parcels, packed, rate, skip = indexed(
        parcel_kernel,
        (shape((rows, parcel_width), bf16),)
        + (shape((rows, width), bf16),) * (CHUNKS - 1)
        + (shape((rows, kv_width), bf16),)
        + (shape((1, heads), f32),) * 2,
        0,
        4 * rows * side,
        [hbm] * 7,
        (whole(rows, parcel_width),)
        + (whole(rows, width),) * (CHUNKS - 1)
        + (whole(rows, kv_width),)
        + (whole(1, heads),) * 2,
        [pltpu.SemaphoreType.DMA((CHUNKS + 6,))],
        PARCEL_VMEM,
    )(
        index_in,
        x,
        maps,
        dt,
        keys[0],
        values[0],
        decay_rate.reshape(1, heads),
        skip_gain.reshape(1, heads),
    )
    got = [lax.ppermute(parcel, "ctx", partner) for parcel in parcels]
    key_values = hand(packed)
    source = hand(source_len)
    query = hand(after(queries[0], key_values, got[0], source))
    pairs = [
        columns,
        lambda chunk: whole(rows, width),
        lambda chunk: mine((half, rows)),
        lambda chunk: fixed((half, rows), 0, (width + 2 * NST) // rows),
        lambda chunk: whole(1, heads),
    ]
    places = lambda chunk: [spec(chunk) for spec in pairs]
    states, firsts, leads, inner = [], [], [], []
    for chunk in range(CHUNKS):
        state, first, lead, both = indexed(
            functools.partial(state_kernel, chunk),
            (shape((NST, width), wire), shape((NST, width), f32)) + (shape((1, width), f32),) * 2,
            4 * rows * NST * width,
            4 * rows * width,
            places(chunk) + [whole(rows, NST), fixed((rows, NST), 0, width // NST)],
            (whole(NST, width),) * 2 + (whole(1, width),) * 2,
        )(index_in, x, got[chunk], dt, got[0], rate, maps, got[0])
        enter = lax.ppermute(state, "ctx", further)
        for _ in range(ctx // 2 - 2):
            enter = jnp.where(index < 2, 0.0, enter.astype(f32))
            enter = lax.ppermute((state.astype(f32) + both * enter).astype(wire), "ctx", further)
        states.append(enter)
        firsts.append(first)
        leads.append(lead)
    nearby = lax.ppermute(after(key_values, firsts[0]), "ctx", partner)
    for chunk in range(CHUNKS):
        inner.append(
            indexed(
                functools.partial(inner_kernel, chunk),
                (shape((rows, width), f32),) * 4,
                8 * rows * rows * width,
                6 * rows * width,
                places(chunk)
                + [
                    whole(1, heads),
                    whole(rows, 2 * NST),
                    fixed((rows, 2 * NST), 0, width // (2 * NST)),
                ],
                (whole(rows, width),) * 4,
            )(index_in, x, got[chunk], dt, got[0], rate, skip, maps, got[0])
        )
    scalar = pl.BlockSpec(memory_space=pltpu.SMEM)


    pieces = [key_values]
    step = ctx // 2
    while step > 1:
        swap = [(i, i ^ step) for i in range(ctx)]
        pieces = pieces + [
            lax.ppermute(after(piece, states[0]), "ctx", swap) for piece in pieces
        ]
        step //= 2
    pieces = pieces + [nearby] + [lax.ppermute(piece, "ctx", partner) for piece in pieces[1:]]
    gated, sums, back = [], [], []
    for chunk in range(CHUNKS):
        some, part, away = indexed(
            outer_kernel,
            (shape((rows, width), bf16), shape((8, rows), f32), shape((rows, width), bf16)),
            4 * rows * rows * width,
            8 * rows * width,
            [whole(NST, width)] * 2
            + [whole(1, width)]
            + [whole(rows, width)] * 4
            + [
                fixed((rows, NST), 0, 1),
                fixed((rows, NST), 0, width // NST + 1),
                columns(chunk),
            ],
            (whole(rows, width), whole(8, rows), whole(rows, width)),
        )(index_in, after(states[chunk], query, nearby) if chunk else after(states[chunk], *[part for parts in inner for part in parts]), firsts[chunk], leads[chunk], *inner[chunk], maps, got[0], gate)
        gated.append(hand(some))
        sums.append(part)
        back.append(lax.ppermute(away, "ctx", partner))
    for chunk in range(CHUNKS):
        some, part = indexed(
            gate_kernel,
            (shape((rows, width), bf16), shape((8, rows), f32)),
            2 * rows * width,
            8 * rows * width,
            [whole(rows, width), others(chunk)],
            (whole(rows, width), whole(8, rows)),
        )(index_in, after(back[chunk], gated[0], gated[1]), gate)
        gated.append(hand(some))
        sums.append(part)
    query_now = after(query, some, *gated[:3])
    spots = lambda first: pl.BlockSpec((rows, HEAD_WIDTH), lambda g: (0, first + g))
    attention = call(
        functools.partial(attention_kernel, ctx),
        shape((rows, groups * wide), bf16),
        4 * rows * wide * groups * ctx * rows,
        8 * rows * wide * groups,
        grid=(groups,),
        in_specs=[scalar, scalar, pl.BlockSpec((rows, wide), lambda g: (0, g))]
        + [spots(0)] * ctx
        + [spots(groups)] * ctx,
        out_specs=pl.BlockSpec((rows, wide), lambda g: (0, g)),
        scratch_shapes=[pltpu.VMEM((ctx * rows, rows), f32)],
    )(index_in, source, query_now, *pieces, *pieces)
    sums = sum(sums)
    swap = [(i, (i + step) % tps) for step in range(1, tps) for i in range(tps)]
    sums = hand(sums + lax.ppermute(sums, "tp", swap))

    mamba = indexed(
        functools.partial(norm_kernel, channels * tps),
        shape((rows, channels), bf16),
        rows * channels,
        4 * rows * channels,
        [whole(rows, width)] * (2 * CHUNKS) + [whole(8, rows), whole(1, channels)],
        whole(rows, channels),
    )(index_in, *gated, sums, norm_gain.reshape(1, channels))
    return (mamba[None], attention[None])


def solution(mesh):
    placed = (
        P("segment", "ctx", "tp"),
        P("segment", "ctx", "tp"),
        P("segment", "ctx", "tp"),
        P("segment", "ctx", None),
        P("tp"),
        P("tp"),
        P("tp"),
        P("segment", "ctx", "tp"),
        P("segment", "ctx", "tp"),
        P("segment", "ctx", "tp"),
        P("segment"),
    )
    return jax.shard_map(
        on_device,
        mesh=mesh,
        in_specs=placed,
        out_specs=(P("segment", "ctx", "tp"), P("segment", "ctx", "tp")),
        check_vma=False,
    )
```

```python
import functools
import math

import jax
import jax.numpy as jnp
from jax import lax
from jax.experimental import pallas as pl
from jax.experimental.pallas import tpu as pltpu
from jax.sharding import PartitionSpec as P

QUERY_HEADS = 64
KEY_VALUE_HEADS = 8
HEAD_WIDTH = 128
NST = 128
HP = 64
GROUP = QUERY_HEADS // KEY_VALUE_HEADS
CHUNKS = 2
VMEM = 16 * 1024 * 1024
PARCEL_VMEM = 60 * 1024 * 1024
HIGH = lax.Precision.HIGHEST


def dot(a, b, dims, precision=None):
    return lax.dot_general(
        a, b, (dims, ((), ())), precision=precision, preferred_element_type=jnp.float32
    )


def call(kernel, out_shape, flops, nbytes, vmem=VMEM, **kw):
    return pl.pallas_call(
        kernel,
        out_shape=out_shape,
        compiler_params=pltpu.CompilerParams(vmem_limit_bytes=vmem),
        cost_estimate=pl.CostEstimate(flops=flops, bytes_accessed=nbytes, transcendentals=0),
        **kw,
    )


def lower_mask(rows):
    return lax.broadcasted_iota(jnp.int32, (rows, rows), 0) >= lax.broadcasted_iota(
        jnp.int32, (rows, rows), 1
    )


def pair_columns(table, pair, rows):
    lane = lax.broadcasted_iota(jnp.int32, (rows, 2 * HP), 1)
    first = jnp.broadcast_to(table[:, 2 * pair : 2 * pair + 1], (rows, 2 * HP))
    second = jnp.broadcast_to(table[:, 2 * pair + 1 : 2 * pair + 2], (rows, 2 * HP))
    return jnp.where(lane < HP, first, second)


def load_kernel(index_ref, x_ref, maps_ref, dt_ref, x_out, maps_out, dt_out, sem):
    side, half = x_out.shape[1], dt_out.shape[0]
    mine = index_ref[0] % 2
    moves = [
        (x_ref.at[:, pl.ds(pl.multiple_of(mine * side, 128), side)], x_out),
        (maps_ref, maps_out),
        (dt_ref.at[pl.ds(pl.multiple_of(mine * half, half), half), :], dt_out),
    ]
    copy_all(moves, sem)


def spread(row, first, width):
    return jnp.concatenate(
        [pair_columns(row, first // 2 + pair, 1) for pair in range(width // (2 * HP))], axis=1
    )


def copy_all(moves, sem):
    copies = [
        pltpu.make_async_copy(src, dst, sem.at[number]) for number, (src, dst) in enumerate(moves)
    ]
    for copy in copies:
        copy.start()
    for copy in copies:
        copy.wait()


def parcel_kernel(
    index_ref, x_ref, maps_ref, dt_ref, key_ref, value_ref, rate_ref, skip_ref, *refs
):
    *parcel_refs, packed_ref, rate_out, skip_out, sem = refs
    rows = x_ref.shape[0]
    side, half = x_ref.shape[1] // 2, dt_ref.shape[0] // 2
    width, kv = side // CHUNKS, key_ref.shape[1]
    away = 1 - index_ref[0] % 2
    first = parcel_refs[0]
    moves = [
        (
            x_ref.at[:, pl.ds(pl.multiple_of(away * side + chunk * width, 128), width)],
            out_ref.at[:, pl.ds(0, width)],
        )
        for chunk, out_ref in enumerate(parcel_refs)
    ]
    moves.append((maps_ref, first.at[:, pl.ds(width, 2 * NST)]))
    moves.append(
        (
            dt_ref.at[pl.ds(pl.multiple_of(away * half, half), half), :],
            first.at[pl.ds(0, half), pl.ds(width + 2 * NST, rows)],
        )
    )
    moves.append((key_ref, packed_ref.at[:, pl.ds(0, kv)]))
    moves.append((value_ref, packed_ref.at[:, pl.ds(kv, kv)]))
    moves.append((rate_ref, rate_out))
    moves.append((skip_ref, skip_out))
    copy_all(moves, sem)


def own_heads(ref, early, chunk, count):
    row = ref[...]
    half = row.shape[1] // 2
    low = row[:, chunk * count : chunk * count + count]
    high = row[:, half + chunk * count : half + chunk * count + count]
    return jnp.where(early, low, high)


def decays(dt, rate, heads):
    rows = dt.shape[1]
    ones = jnp.where(lower_mask(rows), 1.0, 0.0).astype(jnp.bfloat16)
    rate_col = jnp.transpose(jnp.broadcast_to(rate, (8, heads)))[:, :1]
    cum = -rate * dot(ones, dt, ((1,), (1,)))
    cum_t = -rate_col * dot(dt, ones, ((1,), (1,)))
    return cum, cum_t


def state_kernel(
    chunk, index_ref, x_ref, x2_ref, dt_ref, dt2_ref, rate_ref, b_ref, b2_ref,
    out_ref, first_ref, lead_ref, both_ref,
):
    rows, width = x_ref.shape
    count = width // HP
    at = slice(chunk * count, chunk * count + count)
    early = index_ref[0] % 2 == 0
    rate = own_heads(rate_ref, early, chunk, count)
    halves = []
    for x, dt, b in ((x_ref, dt_ref, b_ref), (x2_ref, dt2_ref, b2_ref)):
        step = dt[at, :]
        cum, _ = decays(step, rate, count)
        total = cum[rows - 1 : rows, :]
        tail = jnp.exp(total - cum) * jnp.transpose(step.astype(jnp.float32))
        xw = jnp.concatenate(
            [
                (
                    x[:, pair * 128 : pair * 128 + 128].astype(jnp.float32)
                    * pair_columns(tail, pair, rows)
                ).astype(jnp.bfloat16)
                for pair in range(width // 128)
            ],
            axis=1,
        )
        halves.append((dot(b[...], xw, ((0,), (0,))), spread(jnp.exp(total), 0, width)))
    (mine, mine_decay), (theirs, theirs_decay) = halves
    first = jnp.where(early, mine, theirs)
    second = jnp.where(early, theirs, mine)
    lead = jnp.where(early, mine_decay, theirs_decay)
    trail = jnp.where(early, theirs_decay, mine_decay)
    out_ref[...] = (first * trail + second).astype(out_ref.dtype)
    first_ref[...] = first
    lead_ref[...] = lead
    both_ref[...] = lead * trail


def inner_kernel(
    chunk, index_ref, x_ref, x2_ref, dt_ref, dt2_ref, rate_ref, skip_ref, maps_ref, maps2_ref,
    out_ref, grow_ref, out2_ref, grow2_ref,
):
    early = index_ref[0] % 2 == 0
    rows, width = x_ref.shape
    count = width // HP
    at = slice(chunk * count, chunk * count + count)
    lane = lax.broadcasted_iota(jnp.int32, (rows, 128), 1)
    rate = own_heads(rate_ref, early, chunk, count)
    skip = own_heads(skip_ref, early, chunk, count)
    for x, dt, maps, out, spread_out in (
        (x_ref, dt_ref, maps_ref, out_ref, grow_ref),
        (x2_ref, dt2_ref, maps2_ref, out2_ref, grow2_ref),
    ):
        gram = dot(maps[:, NST:], maps[:, :NST], ((1,), (1,)))
        gram = jnp.where(lower_mask(rows), gram, 0.0)
        step = dt[at, :]
        cum, cum_t = decays(step, rate, count)
        step = step.astype(jnp.float32)
        grow = jnp.exp(cum)
        for pair in range(width // 128):
            mixes = []
            for head in (2 * pair, 2 * pair + 1):
                mine = jnp.broadcast_to(cum[:, head : head + 1], (rows, rows))
                decay = jnp.exp(jnp.minimum(mine - cum_t[head : head + 1, :], 0.0))
                mixes.append((gram * decay * step[head : head + 1, :]).astype(jnp.bfloat16))
            xs = x[:, pair * 128 : pair * 128 + 128]
            zero = jnp.zeros_like(xs)
            stacked = jnp.concatenate(
                [jnp.where(lane < HP, xs, zero), jnp.where(lane < HP, zero, xs)], axis=0
            )
            mixed = dot(jnp.concatenate(mixes, axis=1), stacked, ((1,), (0,)))
            mixed = mixed + pair_columns(skip, pair, 1) * xs.astype(jnp.float32)
            out[:, pair * 128 : pair * 128 + 128] = mixed
            spread_out[:, pair * 128 : pair * 128 + 128] = pair_columns(grow, pair, rows)


def gate_and_sum(raw, gate, out_ref, sums_ref):
    rows, width = raw.shape
    gate = gate.astype(jnp.float32)
    gated = raw.astype(jnp.float32) * (gate / (1.0 + jnp.exp(-gate)))
    out_ref[...] = gated.astype(jnp.bfloat16)
    squares = gated * gated
    total = squares[:, :128]
    for tile in range(1, width // 128):
        total = total + squares[:, tile * 128 : tile * 128 + 128]
    sums_ref[...] = dot(jnp.ones((8, 128), jnp.float32), total, ((1,), (1,)), HIGH)


def outer_kernel(
    index_ref, enter_ref, first_ref, lead_ref, local_ref, grow_ref, local2_ref, grow2_ref,
    c_ref, c2_ref, gate_ref, out_ref, sums_ref, back_ref,
):
    early = index_ref[0] % 2 == 0
    enter = jnp.where(index_ref[0] < 2, 0.0, enter_ref[...].astype(jnp.float32))
    later = lead_ref[...] * enter + first_ref[...]
    mine = jnp.where(early, enter, later).astype(jnp.bfloat16)
    theirs = jnp.where(early, later, enter).astype(jnp.bfloat16)
    back = local2_ref[...] + grow2_ref[...] * dot(c2_ref[...], theirs, ((1,), (0,)))
    back_ref[...] = back.astype(jnp.bfloat16)
    raw = local_ref[...] + grow_ref[...] * dot(c_ref[...], mine, ((1,), (0,)))
    gate_and_sum(raw.astype(jnp.bfloat16), gate_ref[...], out_ref, sums_ref)


def gate_kernel(index_ref, raw_ref, gate_ref, out_ref, sums_ref):
    del index_ref
    gate_and_sum(raw_ref[...], gate_ref[...], out_ref, sums_ref)


def norm_kernel(channels, index_ref, *refs):
    *chunk_refs, sums_ref, gain_ref, out_ref = refs
    rows = out_ref.shape[0]
    half = out_ref.shape[1] // 2
    mean = sums_ref[0:1, :] / channels
    scale = jnp.broadcast_to(lax.rsqrt(mean + 1e-05), (rows, rows))
    eye = lax.broadcasted_iota(jnp.int32, (rows, rows), 0) == lax.broadcasted_iota(
        jnp.int32, (rows, rows), 1
    )
    scale = jnp.sum(jnp.where(eye, scale, 0.0), axis=1, keepdims=True)
    parity = index_ref[0] % 2
    for number, ref in enumerate(chunk_refs):
        width = ref.shape[1]
        side, chunk = divmod(number, CHUNKS)
        start = (parity if side == 0 else 1 - parity) * half + chunk * width
        at = pl.ds(pl.multiple_of(start, 128), width)
        out_ref[:, at] = (ref[...].astype(jnp.float32) * scale * gain_ref[:, at]).astype(
            jnp.bfloat16
        )


def attention_kernel(offsets, index_ref, source_ref, q_ref, *refs):
    blocks = len(offsets)
    key_refs, value_refs, rest = refs[:blocks], refs[blocks : 2 * blocks], refs[2 * blocks :]
    bias_ref = rest[-1]
    rows = q_ref.shape[0]
    index = index_ref[0]
    source = source_ref[0]
    query_pos = index * rows + lax.broadcasted_iota(jnp.int32, (rows, rows), 1)
    for block, offset in enumerate(offsets):
        key_pos = (index ^ offset) * rows + lax.broadcasted_iota(jnp.int32, (rows, rows), 0)
        bias_ref[block * rows : block * rows + rows, :] = jnp.where(
            (key_pos <= query_pos) | (key_pos < source), 0.0, -jnp.inf
        )
    factor = math.log2(math.e) / math.sqrt(HEAD_WIDTH)
    span = lambda head: slice(head * HEAD_WIDTH, (head + 1) * HEAD_WIDTH)
    part = lambda head: slice(head * rows, (head + 1) * rows)
    query = jnp.concatenate([q_ref[:, span(head)] for head in range(GROUP)], axis=0)
    key = jnp.concatenate([ref[...] for ref in key_refs], axis=0)
    value = jnp.concatenate([ref[...] for ref in value_refs], axis=0)
    value = jnp.transpose(value.astype(jnp.float32)).astype(jnp.bfloat16)
    scores = dot(key, query, ((1,), (1,)))
    last = len(rest) == 4
    weights, totals, tops, olds = [], [], [], []
    for head in range(GROUP):
        kept = scores[:, part(head)] + bias_ref[...]
        top = jnp.max(kept, axis=0, keepdims=True)
        if last:
            before = rest[1][0, 0:1, part(head)]
            top = jnp.maximum(top, before)
        weight = jnp.exp2((kept - top) * factor)
        total = jnp.sum(weight, axis=0, keepdims=True)
        if last:
            old = jnp.exp2((before - top) * factor)
            total = total + rest[1][0, 1:2, part(head)] * old
            olds.append(old)
        tops.append(top)
        totals.append(total)
        weights.append(weight.astype(jnp.bfloat16))
    mixed = dot(value, jnp.concatenate(weights, axis=1), ((1,), (0,)))
    if not last:
        rest[0][0] = mixed
        rest[1][0, 0:1, :] = jnp.concatenate(tops, axis=1)
        rest[1][0, 1:2, :] = jnp.concatenate(totals, axis=1)
        return
    mixed = (mixed + rest[0][0] * jnp.concatenate(olds, axis=1)) / jnp.concatenate(totals, axis=1)
    for head in range(GROUP):
        rest[2][:, span(head)] = jnp.transpose(mixed[:, part(head)]).astype(jnp.bfloat16)


def on_device(
    mamba_input,
    mamba_gate,
    step_size,
    state_maps,
    decay_rate,
    skip_gain,
    norm_gain,
    queries,
    keys,
    values,
    source_len,
):
    segments = lax.axis_size("segment")
    ctx = lax.axis_size("ctx")
    tps = lax.axis_size("tp")
    index = lax.axis_index("ctx")
    index_in = index.astype(jnp.int32).reshape(1)
    onward = [(i, (i + 1) % segments) for i in range(segments)]
    partner = [(i, i + 1 - 2 * (i % 2)) for i in range(ctx)]
    further = [(i, (i + 2) % ctx) for i in range(ctx)]
    bf16, f32 = jnp.bfloat16, jnp.float32
    shape = jax.ShapeDtypeStruct

    def hand(array):
        return lax.ppermute(array, "segment", onward)

    def after(value, *others):
        return lax.optimization_barrier((value, *others))[0]

    x, gate, maps = mamba_input[0], mamba_gate[0], state_maps[0]
    dt = step_size[0].T
    heads, rows = dt.shape
    channels = x.shape[1]
    half = heads // 2
    side = channels // 2
    width = side // CHUNKS
    wire = bf16 if ctx <= 8 else f32
    groups = keys.shape[2] // HEAD_WIDTH
    wide = GROUP * HEAD_WIDTH

    whole = lambda *dims: pl.BlockSpec(dims, lambda i, s: (0,) * len(dims))
    fixed = lambda dims, *at: pl.BlockSpec(dims, lambda i, s: at)
    columns = lambda chunk: pl.BlockSpec(
        (rows, width), lambda i, s: (0, (s[0] % 2) * CHUNKS + chunk)
    )
    others = lambda chunk: pl.BlockSpec(
        (rows, width), lambda i, s: (0, (1 - s[0] % 2) * CHUNKS + chunk)
    )

    def indexed(kernel, out_shape, flops, nbytes, in_specs, out_specs, scratch=(), vmem=VMEM):
        return pl.pallas_call(
            kernel,
            out_shape=out_shape,
            grid_spec=pltpu.PrefetchScalarGridSpec(
                num_scalar_prefetch=1,
                grid=(1,),
                in_specs=in_specs,
                out_specs=out_specs,
                scratch_shapes=scratch,
            ),
            compiler_params=pltpu.CompilerParams(vmem_limit_bytes=vmem),
            cost_estimate=pl.CostEstimate(flops=flops, bytes_accessed=nbytes, transcendentals=0),
        )

    parcel_width = width + 2 * NST + rows
    hbm = pl.BlockSpec(memory_space=pltpu.HBM)
    kv_width = 2 * groups * HEAD_WIDTH
    *parcels, packed, rate, skip = indexed(
        parcel_kernel,
        (shape((rows, parcel_width), bf16),)
        + (shape((rows, width), bf16),) * (CHUNKS - 1)
        + (shape((rows, kv_width), bf16),)
        + (shape((1, heads), f32),) * 2,
        0,
        4 * rows * side,
        [hbm] * 7,
        (whole(rows, parcel_width),)
        + (whole(rows, width),) * (CHUNKS - 1)
        + (whole(rows, kv_width),)
        + (whole(1, heads),) * 2,
        [pltpu.SemaphoreType.DMA((CHUNKS + 6,))],
        PARCEL_VMEM,
    )(
        index_in,
        x,
        maps,
        dt,
        keys[0],
        values[0],
        decay_rate.reshape(1, heads),
        skip_gain.reshape(1, heads),
    )
    got = [lax.ppermute(parcel, "ctx", partner) for parcel in parcels]
    key_values = hand(packed)
    source = hand(source_len)
    x_own, maps_own, dt_own = indexed(
        load_kernel,
        (shape((rows, side), bf16), shape((rows, 2 * NST), bf16), shape((half, rows), bf16)),
        0,
        4 * rows * side,
        [hbm] * 3,
        (whole(rows, side), whole(rows, 2 * NST), whole(half, rows)),
        [pltpu.SemaphoreType.DMA((3,))],
        VMEM,
    )(after(index_in, parcels[0]), x, maps, dt)
    query = hand(after(queries[0], key_values, got[0], source, x_own))
    pairs = [
        lambda chunk: fixed((rows, width), 0, chunk),
        lambda chunk: whole(rows, width),
        lambda chunk: whole(half, rows),
        lambda chunk: fixed((half, rows), 0, (width + 2 * NST) // rows),
        lambda chunk: whole(1, heads),
    ]
    places = lambda chunk: [spec(chunk) for spec in pairs]
    states, firsts, leads, inner = [], [], [], []
    for chunk in range(CHUNKS):
        state, first, lead, both = indexed(
            functools.partial(state_kernel, chunk),
            (shape((NST, width), wire), shape((NST, width), f32)) + (shape((1, width), f32),) * 2,
            4 * rows * NST * width,
            4 * rows * width,
            places(chunk) + [whole(rows, NST), fixed((rows, NST), 0, width // NST)],
            (whole(NST, width),) * 2 + (whole(1, width),) * 2,
        )(index_in, x_own, got[chunk], dt_own, got[0], rate, maps_own, got[0])
        enter = lax.ppermute(state, "ctx", further)
        for _ in range(ctx // 2 - 2):
            enter = jnp.where(index < 2, 0.0, enter.astype(f32))
            enter = lax.ppermute((state.astype(f32) + both * enter).astype(wire), "ctx", further)
        states.append(enter)
        firsts.append(first)
        leads.append(lead)
    nearby = lax.ppermute(after(key_values, firsts[0]), "ctx", partner)
    for chunk in range(CHUNKS):
        inner.append(
            indexed(
                functools.partial(inner_kernel, chunk),
                (shape((rows, width), f32),) * 4,
                8 * rows * rows * width,
                6 * rows * width,
                places(chunk)
                + [
                    whole(1, heads),
                    whole(rows, 2 * NST),
                    fixed((rows, 2 * NST), 0, width // (2 * NST)),
                ],
                (whole(rows, width),) * 4,
            )(index_in, x_own, got[chunk], dt_own, got[0], rate, skip, maps_own, got[0])
        )
    scalar = pl.BlockSpec(memory_space=pltpu.SMEM)


    pieces, offsets = [key_values], [0]
    step = ctx // 2
    while step > 1:
        swap = [(i, i ^ step) for i in range(ctx)]
        pieces = pieces + [
            lax.ppermute(after(piece, states[0]), "ctx", swap) for piece in pieces
        ]
        offsets = offsets + [offset ^ step for offset in offsets]
        step //= 2
    far_pieces = pieces[1:] + [lax.ppermute(piece, "ctx", partner) for piece in pieces[1:]]
    far_offsets = offsets[1:] + [offset ^ 1 for offset in offsets[1:]]

    def attend(query, pieces, offsets, more, out_shape, out_specs):
        spots = lambda first: pl.BlockSpec((rows, HEAD_WIDTH), lambda g: (0, first + g))
        return call(
            functools.partial(attention_kernel, offsets),
            out_shape,
            4 * rows * wide * groups * len(offsets) * rows,
            8 * rows * wide * groups,
            VMEM + 8 * len(offsets) * rows * GROUP * rows,
            grid=(groups,),
            in_specs=[scalar, scalar, pl.BlockSpec((rows, wide), lambda g: (0, g))]
            + [spots(0)] * len(offsets)
            + [spots(groups)] * len(offsets)
            + (halves if more else []),
            out_specs=out_specs,
            scratch_shapes=[pltpu.VMEM((len(offsets) * rows, rows), f32)],
        )(index_in, source, query, *pieces, *pieces, *more)

    halves = [
        pl.BlockSpec((1, HEAD_WIDTH, GROUP * rows), lambda g: (g, 0, 0)),
        pl.BlockSpec((1, 2, GROUP * rows), lambda g: (g, 0, 0)),
    ]
    gated, sums, back = [], [], []
    for chunk in range(CHUNKS):
        some, part, away = indexed(
            outer_kernel,
            (shape((rows, width), bf16), shape((8, rows), f32), shape((rows, width), bf16)),
            4 * rows * rows * width,
            8 * rows * width,
            [whole(NST, width)] * 2
            + [whole(1, width)]
            + [whole(rows, width)] * 4
            + [
                fixed((rows, NST), 0, 1),
                fixed((rows, NST), 0, width // NST + 1),
                columns(chunk),
            ],
            (whole(rows, width), whole(8, rows), whole(rows, width)),
        )(index_in, after(states[chunk], query, nearby) if chunk else after(states[chunk], *[part for parts in inner for part in parts]), firsts[chunk], leads[chunk], *inner[chunk], maps_own, got[0], gate)
        gated.append(hand(some))
        sums.append(part)
        back.append(lax.ppermute(away, "ctx", partner))
    near = attend(
        after(query, some),
        [key_values, nearby],
        [0, 1],
        (),
        (
            shape((groups, HEAD_WIDTH, GROUP * rows), f32),
            shape((groups, 2, GROUP * rows), f32),
        ),
        tuple(halves),
    )
    for chunk in range(CHUNKS):
        some, part = indexed(
            gate_kernel,
            (shape((rows, width), bf16), shape((8, rows), f32)),
            2 * rows * width,
            8 * rows * width,
            [whole(rows, width), others(chunk)],
            (whole(rows, width), whole(8, rows)),
        )(index_in, after(back[chunk], gated[0], gated[1], *near), gate)
        gated.append(hand(some))
        sums.append(part)
    attention = attend(
        after(query, some, *gated[:3]),
        far_pieces,
        far_offsets,
        near,
        shape((rows, groups * wide), bf16),
        pl.BlockSpec((rows, wide), lambda g: (0, g)),
    )
    sums = sum(sums)
    swap = [(i, (i + step) % tps) for step in range(1, tps) for i in range(tps)]
    sums = hand(sums + lax.ppermute(sums, "tp", swap))

    mamba = indexed(
        functools.partial(norm_kernel, channels * tps),
        shape((rows, channels), bf16),
        rows * channels,
        4 * rows * channels,
        [whole(rows, width)] * (2 * CHUNKS) + [whole(8, rows), whole(1, channels)],
        whole(rows, channels),
    )(index_in, *gated, sums, norm_gain.reshape(1, channels))
    return (mamba[None], attention[None])


def solution(mesh):
    placed = (
        P("segment", "ctx", "tp"),
        P("segment", "ctx", "tp"),
        P("segment", "ctx", "tp"),
        P("segment", "ctx", None),
        P("tp"),
        P("tp"),
        P("tp"),
        P("segment", "ctx", "tp"),
        P("segment", "ctx", "tp"),
        P("segment", "ctx", "tp"),
        P("segment"),
    )
    return jax.shard_map(
        on_device,
        mesh=mesh,
        in_specs=placed,
        out_specs=(P("segment", "ctx", "tp"), P("segment", "ctx", "tp")),
        check_vma=False,
    )
```

```python
import functools
import math

import jax
import jax.numpy as jnp
from jax import lax
from jax.experimental import pallas as pl
from jax.experimental.pallas import tpu as pltpu
from jax.sharding import PartitionSpec as P

QUERY_HEADS = 64
KEY_VALUE_HEADS = 8
HEAD_WIDTH = 128
NST = 128
HP = 64
GROUP = QUERY_HEADS // KEY_VALUE_HEADS
CHUNKS = 2
VMEM = 16 * 1024 * 1024
PARCEL_VMEM = 60 * 1024 * 1024
HIGH = lax.Precision.HIGHEST


def dot(a, b, dims, precision=None):
    return lax.dot_general(
        a, b, (dims, ((), ())), precision=precision, preferred_element_type=jnp.float32
    )


def call(kernel, out_shape, flops, nbytes, vmem=VMEM, **kw):
    return pl.pallas_call(
        kernel,
        out_shape=out_shape,
        compiler_params=pltpu.CompilerParams(vmem_limit_bytes=vmem),
        cost_estimate=pl.CostEstimate(flops=flops, bytes_accessed=nbytes, transcendentals=0),
        **kw,
    )


def lower_mask(rows):
    return lax.broadcasted_iota(jnp.int32, (rows, rows), 0) >= lax.broadcasted_iota(
        jnp.int32, (rows, rows), 1
    )


def pair_columns(table, pair, rows):
    lane = lax.broadcasted_iota(jnp.int32, (rows, 2 * HP), 1)
    first = jnp.broadcast_to(table[:, 2 * pair : 2 * pair + 1], (rows, 2 * HP))
    second = jnp.broadcast_to(table[:, 2 * pair + 1 : 2 * pair + 2], (rows, 2 * HP))
    return jnp.where(lane < HP, first, second)


def load_kernel(index_ref, x_ref, maps_ref, dt_ref, x_out, maps_out, dt_out, sem):
    side, half = x_out.shape[1], dt_out.shape[0]
    mine = index_ref[0] % 2
    moves = [
        (x_ref.at[:, pl.ds(pl.multiple_of(mine * side, 128), side)], x_out),
        (maps_ref, maps_out),
        (dt_ref.at[pl.ds(pl.multiple_of(mine * half, half), half), :], dt_out),
    ]
    copy_all(moves, sem)


def spread(row, first, width):
    return jnp.concatenate(
        [pair_columns(row, first // 2 + pair, 1) for pair in range(width // (2 * HP))], axis=1
    )


def copy_all(moves, sem):
    copies = [
        pltpu.make_async_copy(src, dst, sem.at[number]) for number, (src, dst) in enumerate(moves)
    ]
    for copy in copies:
        copy.start()
    for copy in copies:
        copy.wait()


def parcel_kernel(
    index_ref, x_ref, maps_ref, dt_ref, key_ref, value_ref, rate_ref, skip_ref, *refs
):
    *parcel_refs, packed_ref, rate_out, skip_out, sem = refs
    rows = x_ref.shape[0]
    side, half = x_ref.shape[1] // 2, dt_ref.shape[0] // 2
    width, kv = side // CHUNKS, key_ref.shape[1]
    away = 1 - index_ref[0] % 2
    first = parcel_refs[0]
    moves = [
        (
            x_ref.at[:, pl.ds(pl.multiple_of(away * side + chunk * width, 128), width)],
            out_ref.at[:, pl.ds(0, width)],
        )
        for chunk, out_ref in enumerate(parcel_refs)
    ]
    moves.append((maps_ref, first.at[:, pl.ds(width, 2 * NST)]))
    moves.append(
        (
            dt_ref.at[pl.ds(pl.multiple_of(away * half, half), half), :],
            first.at[pl.ds(0, half), pl.ds(width + 2 * NST, rows)],
        )
    )
    moves.append((key_ref, packed_ref.at[:, pl.ds(0, kv)]))
    moves.append((value_ref, packed_ref.at[:, pl.ds(kv, kv)]))
    moves.append((rate_ref, rate_out))
    moves.append((skip_ref, skip_out))
    copy_all(moves, sem)


def own_heads(ref, early, chunk, count):
    row = ref[...]
    half = row.shape[1] // 2
    low = row[:, chunk * count : chunk * count + count]
    high = row[:, half + chunk * count : half + chunk * count + count]
    return jnp.where(early, low, high)


def decays(dt, rate, heads):
    rows = dt.shape[1]
    ones = jnp.where(lower_mask(rows), 1.0, 0.0).astype(jnp.bfloat16)
    rate_col = jnp.transpose(jnp.broadcast_to(rate, (8, heads)))[:, :1]
    cum = -rate * dot(ones, dt, ((1,), (1,)))
    cum_t = -rate_col * dot(dt, ones, ((1,), (1,)))
    return cum, cum_t


def state_kernel(
    chunk, index_ref, x_ref, x2_ref, dt_ref, dt2_ref, rate_ref, b_ref, b2_ref,
    out_ref, first_ref, lead_ref, both_ref,
):
    rows, width = x_ref.shape
    count = width // HP
    at = slice(chunk * count, chunk * count + count)
    early = index_ref[0] % 2 == 0
    rate = own_heads(rate_ref, early, chunk, count)
    halves = []
    for x, dt, b in ((x_ref, dt_ref, b_ref), (x2_ref, dt2_ref, b2_ref)):
        step = dt[at, :]
        cum, _ = decays(step, rate, count)
        total = cum[rows - 1 : rows, :]
        tail = jnp.exp(total - cum) * jnp.transpose(step.astype(jnp.float32))
        xw = jnp.concatenate(
            [
                (
                    x[:, pair * 128 : pair * 128 + 128].astype(jnp.float32)
                    * pair_columns(tail, pair, rows)
                ).astype(jnp.bfloat16)
                for pair in range(width // 128)
            ],
            axis=1,
        )
        halves.append((dot(b[...], xw, ((0,), (0,))), spread(jnp.exp(total), 0, width)))
    (mine, mine_decay), (theirs, theirs_decay) = halves
    first = jnp.where(early, mine, theirs)
    second = jnp.where(early, theirs, mine)
    lead = jnp.where(early, mine_decay, theirs_decay)
    trail = jnp.where(early, theirs_decay, mine_decay)
    out_ref[...] = (first * trail + second).astype(out_ref.dtype)
    first_ref[...] = first
    lead_ref[...] = lead
    both_ref[...] = lead * trail


def inner_kernel(
    chunk, index_ref, x_ref, x2_ref, dt_ref, dt2_ref, rate_ref, skip_ref, maps_ref, maps2_ref,
    out_ref, grow_ref, out2_ref, grow2_ref,
):
    early = index_ref[0] % 2 == 0
    rows, width = x_ref.shape
    count = width // HP
    at = slice(chunk * count, chunk * count + count)
    lane = lax.broadcasted_iota(jnp.int32, (rows, 128), 1)
    rate = own_heads(rate_ref, early, chunk, count)
    skip = own_heads(skip_ref, early, chunk, count)
    for x, dt, maps, out, spread_out in (
        (x_ref, dt_ref, maps_ref, out_ref, grow_ref),
        (x2_ref, dt2_ref, maps2_ref, out2_ref, grow2_ref),
    ):
        gram = dot(maps[:, NST:], maps[:, :NST], ((1,), (1,)))
        gram = jnp.where(lower_mask(rows), gram, 0.0)
        step = dt[at, :]
        cum, cum_t = decays(step, rate, count)
        step = step.astype(jnp.float32)
        grow = jnp.exp(cum)
        for pair in range(width // 128):
            mixes = []
            for head in (2 * pair, 2 * pair + 1):
                mine = jnp.broadcast_to(cum[:, head : head + 1], (rows, rows))
                decay = jnp.exp(jnp.minimum(mine - cum_t[head : head + 1, :], 0.0))
                mixes.append((gram * decay * step[head : head + 1, :]).astype(jnp.bfloat16))
            xs = x[:, pair * 128 : pair * 128 + 128]
            zero = jnp.zeros_like(xs)
            stacked = jnp.concatenate(
                [jnp.where(lane < HP, xs, zero), jnp.where(lane < HP, zero, xs)], axis=0
            )
            mixed = dot(jnp.concatenate(mixes, axis=1), stacked, ((1,), (0,)))
            mixed = mixed + pair_columns(skip, pair, 1) * xs.astype(jnp.float32)
            out[:, pair * 128 : pair * 128 + 128] = mixed
            spread_out[:, pair * 128 : pair * 128 + 128] = pair_columns(grow, pair, rows)


def gate_and_sum(raw, gate, out_ref, sums_ref):
    rows, width = raw.shape
    gate = gate.astype(jnp.float32)
    gated = raw.astype(jnp.float32) * (gate / (1.0 + jnp.exp(-gate)))
    out_ref[...] = gated.astype(jnp.bfloat16)
    squares = gated * gated
    total = squares[:, :128]
    for tile in range(1, width // 128):
        total = total + squares[:, tile * 128 : tile * 128 + 128]
    sums_ref[...] = dot(jnp.ones((8, 128), jnp.float32), total, ((1,), (1,)), HIGH)


def outer_kernel(
    index_ref, enter_ref, first_ref, lead_ref, local_ref, grow_ref, local2_ref, grow2_ref,
    c_ref, c2_ref, gate_ref, out_ref, sums_ref, back_ref,
):
    early = index_ref[0] % 2 == 0
    enter = jnp.where(index_ref[0] < 2, 0.0, enter_ref[...].astype(jnp.float32))
    later = lead_ref[...] * enter + first_ref[...]
    mine = jnp.where(early, enter, later).astype(jnp.bfloat16)
    theirs = jnp.where(early, later, enter).astype(jnp.bfloat16)
    back = local2_ref[...] + grow2_ref[...] * dot(c2_ref[...], theirs, ((1,), (0,)))
    back_ref[...] = back.astype(jnp.bfloat16)
    raw = local_ref[...] + grow_ref[...] * dot(c_ref[...], mine, ((1,), (0,)))
    gate_and_sum(raw.astype(jnp.bfloat16), gate_ref[...], out_ref, sums_ref)


def gate_kernel(index_ref, raw_ref, gate_ref, out_ref, sums_ref):
    del index_ref
    gate_and_sum(raw_ref[...], gate_ref[...], out_ref, sums_ref)


def norm_kernel(channels, index_ref, *refs):
    *chunk_refs, sums_ref, gain_ref, out_ref = refs
    rows = out_ref.shape[0]
    half = out_ref.shape[1] // 2
    mean = sums_ref[0:1, :] / channels
    scale = jnp.broadcast_to(lax.rsqrt(mean + 1e-05), (rows, rows))
    eye = lax.broadcasted_iota(jnp.int32, (rows, rows), 0) == lax.broadcasted_iota(
        jnp.int32, (rows, rows), 1
    )
    scale = jnp.sum(jnp.where(eye, scale, 0.0), axis=1, keepdims=True)
    parity = index_ref[0] % 2
    for number, ref in enumerate(chunk_refs):
        width = ref.shape[1]
        side, chunk = divmod(number, CHUNKS)
        start = (parity if side == 0 else 1 - parity) * half + chunk * width
        at = pl.ds(pl.multiple_of(start, 128), width)
        out_ref[:, at] = (ref[...].astype(jnp.float32) * scale * gain_ref[:, at]).astype(
            jnp.bfloat16
        )


def attention_kernel(offsets, index_ref, source_ref, q_ref, *refs):
    blocks = len(offsets)
    key_refs, value_refs, rest = refs[:blocks], refs[blocks : 2 * blocks], refs[2 * blocks :]
    bias_ref = rest[-1]
    rows = q_ref.shape[0]
    index = index_ref[0]
    source = source_ref[0]
    query_pos = index * rows + lax.broadcasted_iota(jnp.int32, (rows, rows), 1)
    for block, offset in enumerate(offsets):
        key_pos = (index ^ offset) * rows + lax.broadcasted_iota(jnp.int32, (rows, rows), 0)
        bias_ref[block * rows : block * rows + rows, :] = jnp.where(
            (key_pos <= query_pos) | (key_pos < source), 0.0, -jnp.inf
        )
    factor = math.log2(math.e) / math.sqrt(HEAD_WIDTH)
    span = lambda head: slice(head * HEAD_WIDTH, (head + 1) * HEAD_WIDTH)
    part = lambda head: slice(head * rows, (head + 1) * rows)
    query = jnp.concatenate([q_ref[:, span(head)] for head in range(GROUP)], axis=0)
    key = jnp.concatenate([ref[...] for ref in key_refs], axis=0)
    value = jnp.concatenate([ref[...] for ref in value_refs], axis=0)
    value = jnp.transpose(value.astype(jnp.float32)).astype(jnp.bfloat16)
    scores = dot(key, query, ((1,), (1,)))
    last = len(rest) == 4
    weights, totals, tops, olds = [], [], [], []
    for head in range(GROUP):
        kept = scores[:, part(head)] + bias_ref[...]
        top = jnp.max(kept, axis=0, keepdims=True)
        if last:
            before = rest[1][0, 0:1, part(head)]
            top = jnp.maximum(top, before)
        weight = jnp.exp2((kept - top) * factor)
        total = jnp.sum(weight, axis=0, keepdims=True)
        if last:
            old = jnp.exp2((before - top) * factor)
            total = total + rest[1][0, 1:2, part(head)] * old
            olds.append(old)
        tops.append(top)
        totals.append(total)
        weights.append(weight.astype(jnp.bfloat16))
    mixed = dot(value, jnp.concatenate(weights, axis=1), ((1,), (0,)))
    if not last:
        rest[0][0] = mixed
        rest[1][0, 0:1, :] = jnp.concatenate(tops, axis=1)
        rest[1][0, 1:2, :] = jnp.concatenate(totals, axis=1)
        return
    mixed = (mixed + rest[0][0] * jnp.concatenate(olds, axis=1)) / jnp.concatenate(totals, axis=1)
    for head in range(GROUP):
        rest[2][:, span(head)] = jnp.transpose(mixed[:, part(head)]).astype(jnp.bfloat16)


def on_device(
    mamba_input,
    mamba_gate,
    step_size,
    state_maps,
    decay_rate,
    skip_gain,
    norm_gain,
    queries,
    keys,
    values,
    source_len,
):
    segments = lax.axis_size("segment")
    ctx = lax.axis_size("ctx")
    tps = lax.axis_size("tp")
    index = lax.axis_index("ctx")
    index_in = index.astype(jnp.int32).reshape(1)
    onward = [(i, (i + 1) % segments) for i in range(segments)]
    partner = [(i, i + 1 - 2 * (i % 2)) for i in range(ctx)]
    further = [(i, (i + 2) % ctx) for i in range(ctx)]
    bf16, f32 = jnp.bfloat16, jnp.float32
    shape = jax.ShapeDtypeStruct

    def hand(array):
        return lax.ppermute(array, "segment", onward)

    def after(value, *others):
        return lax.optimization_barrier((value, *others))[0]

    x, gate, maps = mamba_input[0], mamba_gate[0], state_maps[0]
    dt = step_size[0].T
    heads, rows = dt.shape
    channels = x.shape[1]
    half = heads // 2
    side = channels // 2
    width = side // CHUNKS
    wire = bf16 if ctx <= 8 else f32
    groups = keys.shape[2] // HEAD_WIDTH
    wide = GROUP * HEAD_WIDTH

    whole = lambda *dims: pl.BlockSpec(dims, lambda i, s: (0,) * len(dims))
    fixed = lambda dims, *at: pl.BlockSpec(dims, lambda i, s: at)
    columns = lambda chunk: pl.BlockSpec(
        (rows, width), lambda i, s: (0, (s[0] % 2) * CHUNKS + chunk)
    )
    others = lambda chunk: pl.BlockSpec(
        (rows, width), lambda i, s: (0, (1 - s[0] % 2) * CHUNKS + chunk)
    )

    def indexed(kernel, out_shape, flops, nbytes, in_specs, out_specs, scratch=(), vmem=VMEM):
        return pl.pallas_call(
            kernel,
            out_shape=out_shape,
            grid_spec=pltpu.PrefetchScalarGridSpec(
                num_scalar_prefetch=1,
                grid=(1,),
                in_specs=in_specs,
                out_specs=out_specs,
                scratch_shapes=scratch,
            ),
            compiler_params=pltpu.CompilerParams(vmem_limit_bytes=vmem),
            cost_estimate=pl.CostEstimate(flops=flops, bytes_accessed=nbytes, transcendentals=0),
        )

    parcel_width = width + 2 * NST + rows
    hbm = pl.BlockSpec(memory_space=pltpu.HBM)
    kv_width = 2 * groups * HEAD_WIDTH
    *parcels, packed, rate, skip = indexed(
        parcel_kernel,
        (shape((rows, parcel_width), bf16),)
        + (shape((rows, width), bf16),) * (CHUNKS - 1)
        + (shape((rows, kv_width), bf16),)
        + (shape((1, heads), f32),) * 2,
        0,
        4 * rows * side,
        [hbm] * 7,
        (whole(rows, parcel_width),)
        + (whole(rows, width),) * (CHUNKS - 1)
        + (whole(rows, kv_width),)
        + (whole(1, heads),) * 2,
        [pltpu.SemaphoreType.DMA((CHUNKS + 6,))],
        PARCEL_VMEM,
    )(
        index_in,
        x,
        maps,
        dt,
        keys[0],
        values[0],
        decay_rate.reshape(1, heads),
        skip_gain.reshape(1, heads),
    )
    got = [lax.ppermute(parcels[0], "ctx", partner)]
    key_values = hand(packed)
    source = hand(source_len)
    x_own, maps_own, dt_own = indexed(
        load_kernel,
        (shape((rows, side), bf16), shape((rows, 2 * NST), bf16), shape((half, rows), bf16)),
        0,
        4 * rows * side,
        [hbm] * 3,
        (whole(rows, side), whole(rows, 2 * NST), whole(half, rows)),
        [pltpu.SemaphoreType.DMA((3,))],
        VMEM,
    )(after(index_in, parcels[0]), x, maps, dt)
    query = hand(after(queries[0], key_values, got[0], source, x_own))
    pairs = [
        lambda chunk: fixed((rows, width), 0, chunk),
        lambda chunk: whole(rows, width),
        lambda chunk: whole(half, rows),
        lambda chunk: fixed((half, rows), 0, (width + 2 * NST) // rows),
        lambda chunk: whole(1, heads),
    ]
    places = lambda chunk: [spec(chunk) for spec in pairs]
    states, firsts, leads, inner = [], [], [], []
    for chunk in range(CHUNKS):
        state, first, lead, both = indexed(
            functools.partial(state_kernel, chunk),
            (shape((NST, width), wire), shape((NST, width), f32)) + (shape((1, width), f32),) * 2,
            4 * rows * NST * width,
            4 * rows * width,
            places(chunk) + [whole(rows, NST), fixed((rows, NST), 0, width // NST)],
            (whole(NST, width),) * 2 + (whole(1, width),) * 2,
        )(index_in, x_own, got[chunk], dt_own, got[0], rate, maps_own, got[0])
        enter = lax.ppermute(state, "ctx", further)
        for _ in range(ctx // 2 - 2):
            enter = jnp.where(index < 2, 0.0, enter.astype(f32))
            enter = lax.ppermute((state.astype(f32) + both * enter).astype(wire), "ctx", further)
        states.append(enter)
        firsts.append(first)
        if chunk + 1 < CHUNKS:
            got.append(lax.ppermute(after(parcels[chunk + 1], first), "ctx", partner))
        leads.append(lead)
    for chunk in range(CHUNKS):
        inner.append(
            indexed(
                functools.partial(inner_kernel, chunk),
                (shape((rows, width), f32),) * 4,
                8 * rows * rows * width,
                6 * rows * width,
                places(chunk)
                + [
                    whole(1, heads),
                    whole(rows, 2 * NST),
                    fixed((rows, 2 * NST), 0, width // (2 * NST)),
                ],
                (whole(rows, width),) * 4,
            )(index_in, x_own, got[chunk], dt_own, got[0], rate, skip, maps_own, got[0])
        )
    scalar = pl.BlockSpec(memory_space=pltpu.SMEM)


    nearby = lax.ppermute(after(key_values, inner[0][0]), "ctx", partner)
    pieces, offsets = [key_values], [0]
    step = ctx // 2
    while step > 1:
        swap = [(i, i ^ step) for i in range(ctx)]
        pieces = pieces + [
            lax.ppermute(after(piece, states[0]), "ctx", swap) for piece in pieces
        ]
        offsets = offsets + [offset ^ step for offset in offsets]
        step //= 2
    far_pieces = pieces[1:] + [lax.ppermute(piece, "ctx", partner) for piece in pieces[1:]]
    far_offsets = offsets[1:] + [offset ^ 1 for offset in offsets[1:]]

    def attend(query, pieces, offsets, more, out_shape, out_specs):
        spots = lambda first: pl.BlockSpec((rows, HEAD_WIDTH), lambda g: (0, first + g))
        return call(
            functools.partial(attention_kernel, offsets),
            out_shape,
            4 * rows * wide * groups * len(offsets) * rows,
            8 * rows * wide * groups,
            VMEM + 8 * len(offsets) * rows * GROUP * rows,
            grid=(groups,),
            in_specs=[scalar, scalar, pl.BlockSpec((rows, wide), lambda g: (0, g))]
            + [spots(0)] * len(offsets)
            + [spots(groups)] * len(offsets)
            + (halves if more else []),
            out_specs=out_specs,
            scratch_shapes=[pltpu.VMEM((len(offsets) * rows, rows), f32)],
        )(index_in, source, query, *pieces, *pieces, *more)

    halves = [
        pl.BlockSpec((1, HEAD_WIDTH, GROUP * rows), lambda g: (g, 0, 0)),
        pl.BlockSpec((1, 2, GROUP * rows), lambda g: (g, 0, 0)),
    ]
    gated, sums, back = [], [], []
    for chunk in range(CHUNKS):
        some, part, away = indexed(
            outer_kernel,
            (shape((rows, width), bf16), shape((8, rows), f32), shape((rows, width), bf16)),
            4 * rows * rows * width,
            8 * rows * width,
            [whole(NST, width)] * 2
            + [whole(1, width)]
            + [whole(rows, width)] * 4
            + [
                fixed((rows, NST), 0, 1),
                fixed((rows, NST), 0, width // NST + 1),
                columns(chunk),
            ],
            (whole(rows, width), whole(8, rows), whole(rows, width)),
        )(index_in, after(states[chunk], query, nearby) if chunk else after(states[chunk], *[part for parts in inner for part in parts]), firsts[chunk], leads[chunk], *inner[chunk], maps_own, got[0], gate)
        gated.append(hand(some))
        sums.append(part)
        back.append(lax.ppermute(away, "ctx", partner))
    near = attend(
        after(query, some),
        [key_values, nearby],
        [0, 1],
        (),
        (
            shape((groups, HEAD_WIDTH, GROUP * rows), f32),
            shape((groups, 2, GROUP * rows), f32),
        ),
        tuple(halves),
    )
    for chunk in range(CHUNKS):
        some, part = indexed(
            gate_kernel,
            (shape((rows, width), bf16), shape((8, rows), f32)),
            2 * rows * width,
            8 * rows * width,
            [whole(rows, width), others(chunk)],
            (whole(rows, width), whole(8, rows)),
        )(index_in, after(back[chunk], gated[0], gated[1], *near), gate)
        gated.append(hand(some))
        sums.append(part)
    attention = attend(
        after(query, some, *gated[:3]),
        far_pieces,
        far_offsets,
        near,
        shape((rows, groups * wide), bf16),
        pl.BlockSpec((rows, wide), lambda g: (0, g)),
    )
    sums = sum(sums)
    swap = [(i, (i + step) % tps) for step in range(1, tps) for i in range(tps)]
    sums = hand(sums + lax.ppermute(sums, "tp", swap))

    mamba = indexed(
        functools.partial(norm_kernel, channels * tps),
        shape((rows, channels), bf16),
        rows * channels,
        4 * rows * channels,
        [whole(rows, width)] * (2 * CHUNKS) + [whole(8, rows), whole(1, channels)],
        whole(rows, channels),
    )(index_in, *gated, sums, norm_gain.reshape(1, channels))
    return (mamba[None], attention[None])


def solution(mesh):
    placed = (
        P("segment", "ctx", "tp"),
        P("segment", "ctx", "tp"),
        P("segment", "ctx", "tp"),
        P("segment", "ctx", None),
        P("tp"),
        P("tp"),
        P("tp"),
        P("segment", "ctx", "tp"),
        P("segment", "ctx", "tp"),
        P("segment", "ctx", "tp"),
        P("segment"),
    )
    return jax.shard_map(
        on_device,
        mesh=mesh,
        in_specs=placed,
        out_specs=(P("segment", "ctx", "tp"), P("segment", "ctx", "tp")),
        check_vma=False,
    )
```

```python
import functools
import math

import jax
import jax.numpy as jnp
from jax import lax
from jax.experimental import pallas as pl
from jax.experimental.pallas import tpu as pltpu
from jax.sharding import PartitionSpec as P

QUERY_HEADS = 64
KEY_VALUE_HEADS = 8
HEAD_WIDTH = 128
NST = 128
HP = 64
GROUP = QUERY_HEADS // KEY_VALUE_HEADS
CHUNKS = 2
VMEM = 16 * 1024 * 1024
PARCEL_VMEM = 60 * 1024 * 1024
HIGH = lax.Precision.HIGHEST


def dot(a, b, dims, precision=None):
    return lax.dot_general(
        a, b, (dims, ((), ())), precision=precision, preferred_element_type=jnp.float32
    )


def call(kernel, out_shape, flops, nbytes, vmem=VMEM, **kw):
    return pl.pallas_call(
        kernel,
        out_shape=out_shape,
        compiler_params=pltpu.CompilerParams(vmem_limit_bytes=vmem),
        cost_estimate=pl.CostEstimate(flops=flops, bytes_accessed=nbytes, transcendentals=0),
        **kw,
    )


def lower_mask(rows):
    return lax.broadcasted_iota(jnp.int32, (rows, rows), 0) >= lax.broadcasted_iota(
        jnp.int32, (rows, rows), 1
    )


def pair_columns(table, pair, rows):
    lane = lax.broadcasted_iota(jnp.int32, (rows, 2 * HP), 1)
    first = jnp.broadcast_to(table[:, 2 * pair : 2 * pair + 1], (rows, 2 * HP))
    second = jnp.broadcast_to(table[:, 2 * pair + 1 : 2 * pair + 2], (rows, 2 * HP))
    return jnp.where(lane < HP, first, second)


def load_kernel(index_ref, x_ref, maps_ref, dt_ref, x_out, maps_out, dt_out, sem):
    side, half = x_out.shape[1], dt_out.shape[0]
    mine = index_ref[0] % 2
    moves = [
        (x_ref.at[:, pl.ds(pl.multiple_of(mine * side, 128), side)], x_out),
        (maps_ref, maps_out),
        (dt_ref.at[pl.ds(pl.multiple_of(mine * half, half), half), :], dt_out),
    ]
    copy_all(moves, sem)


def spread(row, first, width):
    return jnp.concatenate(
        [pair_columns(row, first // 2 + pair, 1) for pair in range(width // (2 * HP))], axis=1
    )


def copy_all(moves, sem):
    copies = [
        pltpu.make_async_copy(src, dst, sem.at[number]) for number, (src, dst) in enumerate(moves)
    ]
    for copy in copies:
        copy.start()
    for copy in copies:
        copy.wait()


def parcel_kernel(
    index_ref, x_ref, maps_ref, dt_ref, key_ref, value_ref, rate_ref, skip_ref, *refs
):
    *parcel_refs, packed_ref, rate_out, skip_out, sem = refs
    rows = x_ref.shape[0]
    side, half = x_ref.shape[1] // 2, dt_ref.shape[0] // 2
    width, kv = side // CHUNKS, key_ref.shape[1]
    away = 1 - index_ref[0] % 2
    first = parcel_refs[0]
    moves = [
        (
            x_ref.at[:, pl.ds(pl.multiple_of(away * side + chunk * width, 128), width)],
            out_ref.at[:, pl.ds(0, width)],
        )
        for chunk, out_ref in enumerate(parcel_refs)
    ]
    moves.append((maps_ref, first.at[:, pl.ds(width, 2 * NST)]))
    moves.append(
        (
            dt_ref.at[pl.ds(pl.multiple_of(away * half, half), half), :],
            first.at[pl.ds(0, half), pl.ds(width + 2 * NST, rows)],
        )
    )
    moves.append((key_ref, packed_ref.at[:, pl.ds(0, kv)]))
    moves.append((value_ref, packed_ref.at[:, pl.ds(kv, kv)]))
    moves.append((rate_ref, rate_out))
    moves.append((skip_ref, skip_out))
    copy_all(moves, sem)


def own_heads(ref, early, chunk, count):
    row = ref[...]
    half = row.shape[1] // 2
    low = row[:, chunk * count : chunk * count + count]
    high = row[:, half + chunk * count : half + chunk * count + count]
    return jnp.where(early, low, high)


def decays(dt, rate, heads):
    rows = dt.shape[1]
    ones = jnp.where(lower_mask(rows), 1.0, 0.0).astype(jnp.bfloat16)
    rate_col = jnp.transpose(jnp.broadcast_to(rate, (8, heads)))[:, :1]
    cum = -rate * dot(ones, dt, ((1,), (1,)))
    cum_t = -rate_col * dot(dt, ones, ((1,), (1,)))
    return cum, cum_t


def state_kernel(
    chunk, index_ref, x_ref, x2_ref, dt_ref, dt2_ref, rate_ref, b_ref, b2_ref,
    out_ref, first_ref, lead_ref, both_ref,
):
    rows, width = x_ref.shape
    count = width // HP
    at = slice(chunk * count, chunk * count + count)
    early = index_ref[0] % 2 == 0
    rate = own_heads(rate_ref, early, chunk, count)
    halves = []
    for x, dt, b in ((x_ref, dt_ref, b_ref), (x2_ref, dt2_ref, b2_ref)):
        step = dt[at, :]
        cum, _ = decays(step, rate, count)
        total = cum[rows - 1 : rows, :]
        tail = jnp.exp(total - cum) * jnp.transpose(step.astype(jnp.float32))
        xw = jnp.concatenate(
            [
                (
                    x[:, pair * 128 : pair * 128 + 128].astype(jnp.float32)
                    * pair_columns(tail, pair, rows)
                ).astype(jnp.bfloat16)
                for pair in range(width // 128)
            ],
            axis=1,
        )
        halves.append((dot(b[...], xw, ((0,), (0,))), spread(jnp.exp(total), 0, width)))
    (mine, mine_decay), (theirs, theirs_decay) = halves
    first = jnp.where(early, mine, theirs)
    second = jnp.where(early, theirs, mine)
    lead = jnp.where(early, mine_decay, theirs_decay)
    trail = jnp.where(early, theirs_decay, mine_decay)
    out_ref[...] = (first * trail + second).astype(out_ref.dtype)
    first_ref[...] = first
    lead_ref[...] = lead
    both_ref[...] = lead * trail


def inner_kernel(
    chunk, index_ref, x_ref, x2_ref, dt_ref, dt2_ref, rate_ref, skip_ref, maps_ref, maps2_ref,
    out_ref, grow_ref, out2_ref, grow2_ref,
):
    early = index_ref[0] % 2 == 0
    rows, width = x_ref.shape
    count = width // HP
    at = slice(chunk * count, chunk * count + count)
    lane = lax.broadcasted_iota(jnp.int32, (rows, 128), 1)
    rate = own_heads(rate_ref, early, chunk, count)
    skip = own_heads(skip_ref, early, chunk, count)
    for x, dt, maps, out, spread_out in (
        (x_ref, dt_ref, maps_ref, out_ref, grow_ref),
        (x2_ref, dt2_ref, maps2_ref, out2_ref, grow2_ref),
    ):
        gram = dot(maps[:, NST:], maps[:, :NST], ((1,), (1,)))
        gram = jnp.where(lower_mask(rows), gram, 0.0)
        step = dt[at, :]
        cum, cum_t = decays(step, rate, count)
        step = step.astype(jnp.float32)
        grow = jnp.exp(cum)
        for pair in range(width // 128):
            mixes = []
            for head in (2 * pair, 2 * pair + 1):
                mine = jnp.broadcast_to(cum[:, head : head + 1], (rows, rows))
                decay = jnp.exp(jnp.minimum(mine - cum_t[head : head + 1, :], 0.0))
                mixes.append((gram * decay * step[head : head + 1, :]).astype(jnp.bfloat16))
            xs = x[:, pair * 128 : pair * 128 + 128]
            zero = jnp.zeros_like(xs)
            stacked = jnp.concatenate(
                [jnp.where(lane < HP, xs, zero), jnp.where(lane < HP, zero, xs)], axis=0
            )
            mixed = dot(jnp.concatenate(mixes, axis=1), stacked, ((1,), (0,)))
            mixed = mixed + pair_columns(skip, pair, 1) * xs.astype(jnp.float32)
            out[:, pair * 128 : pair * 128 + 128] = mixed
            spread_out[:, pair * 128 : pair * 128 + 128] = pair_columns(grow, pair, rows)


def gate_and_sum(raw, gate, out_ref, sums_ref):
    rows, width = raw.shape
    gate = gate.astype(jnp.float32)
    gated = raw.astype(jnp.float32) * (gate / (1.0 + jnp.exp(-gate)))
    out_ref[...] = gated.astype(jnp.bfloat16)
    squares = gated * gated
    total = squares[:, :128]
    for tile in range(1, width // 128):
        total = total + squares[:, tile * 128 : tile * 128 + 128]
    sums_ref[...] = dot(jnp.ones((8, 128), jnp.float32), total, ((1,), (1,)), HIGH)


def outer_kernel(
    index_ref, enter_ref, first_ref, lead_ref, local_ref, grow_ref, local2_ref, grow2_ref,
    c_ref, c2_ref, gate_ref, out_ref, sums_ref, back_ref,
):
    early = index_ref[0] % 2 == 0
    enter = jnp.where(index_ref[0] < 2, 0.0, enter_ref[...].astype(jnp.float32))
    later = lead_ref[...] * enter + first_ref[...]
    mine = jnp.where(early, enter, later).astype(jnp.bfloat16)
    theirs = jnp.where(early, later, enter).astype(jnp.bfloat16)
    back = local2_ref[...] + grow2_ref[...] * dot(c2_ref[...], theirs, ((1,), (0,)))
    back_ref[...] = back.astype(jnp.bfloat16)
    raw = local_ref[...] + grow_ref[...] * dot(c_ref[...], mine, ((1,), (0,)))
    gate_and_sum(raw.astype(jnp.bfloat16), gate_ref[...], out_ref, sums_ref)


def gate_kernel(index_ref, raw_ref, gate_ref, out_ref, sums_ref):
    del index_ref
    gate_and_sum(raw_ref[...], gate_ref[...], out_ref, sums_ref)


def norm_kernel(channels, index_ref, *refs):
    *chunk_refs, sums_ref, gain_ref, out_ref = refs
    rows = out_ref.shape[0]
    half = out_ref.shape[1] // 2
    mean = sums_ref[0:1, :] / channels
    scale = jnp.broadcast_to(lax.rsqrt(mean + 1e-05), (rows, rows))
    eye = lax.broadcasted_iota(jnp.int32, (rows, rows), 0) == lax.broadcasted_iota(
        jnp.int32, (rows, rows), 1
    )
    scale = jnp.sum(jnp.where(eye, scale, 0.0), axis=1, keepdims=True)
    parity = index_ref[0] % 2
    for number, ref in enumerate(chunk_refs):
        width = ref.shape[1]
        side, chunk = divmod(number, CHUNKS)
        start = (parity if side == 0 else 1 - parity) * half + chunk * width
        at = pl.ds(pl.multiple_of(start, 128), width)
        out_ref[:, at] = (ref[...].astype(jnp.float32) * scale * gain_ref[:, at]).astype(
            jnp.bfloat16
        )


def attention_kernel(offsets, index_ref, source_ref, q_ref, *refs):
    blocks = len(offsets)
    key_refs, value_refs, rest = refs[:blocks], refs[blocks : 2 * blocks], refs[2 * blocks :]
    bias_ref = rest[-1]
    rows = q_ref.shape[0]
    index = index_ref[0]
    source = source_ref[0]
    query_pos = index * rows + lax.broadcasted_iota(jnp.int32, (rows, rows), 1)
    for block, offset in enumerate(offsets):
        key_pos = (index ^ offset) * rows + lax.broadcasted_iota(jnp.int32, (rows, rows), 0)
        bias_ref[block * rows : block * rows + rows, :] = jnp.where(
            (key_pos <= query_pos) | (key_pos < source), 0.0, -jnp.inf
        )
    factor = math.log2(math.e) / math.sqrt(HEAD_WIDTH)
    span = lambda head: slice(head * HEAD_WIDTH, (head + 1) * HEAD_WIDTH)
    part = lambda head: slice(head * rows, (head + 1) * rows)
    query = jnp.concatenate([q_ref[:, span(head)] for head in range(GROUP)], axis=0)
    key = jnp.concatenate([ref[...] for ref in key_refs], axis=0)
    value = jnp.concatenate([ref[...] for ref in value_refs], axis=0)
    value = jnp.transpose(value.astype(jnp.float32)).astype(jnp.bfloat16)
    scores = dot(key, query, ((1,), (1,)))
    last = len(rest) == 4
    weights, totals, tops, olds = [], [], [], []
    for head in range(GROUP):
        kept = scores[:, part(head)] + bias_ref[...]
        top = jnp.max(kept, axis=0, keepdims=True)
        if last:
            before = rest[1][0, 0:1, part(head)]
            top = jnp.maximum(top, before)
        weight = jnp.exp2((kept - top) * factor)
        total = jnp.sum(weight, axis=0, keepdims=True)
        if last:
            old = jnp.exp2((before - top) * factor)
            total = total + rest[1][0, 1:2, part(head)] * old
            olds.append(old)
        tops.append(top)
        totals.append(total)
        weights.append(weight.astype(jnp.bfloat16))
    mixed = dot(value, jnp.concatenate(weights, axis=1), ((1,), (0,)))
    if not last:
        rest[0][0] = mixed
        rest[1][0, 0:1, :] = jnp.concatenate(tops, axis=1)
        rest[1][0, 1:2, :] = jnp.concatenate(totals, axis=1)
        return
    scale = 1.0 / jnp.concatenate(totals, axis=1)
    mixed = mixed * scale + rest[0][0] * (jnp.concatenate(olds, axis=1) * scale)
    for head in range(GROUP):
        rest[2][:, span(head)] = jnp.transpose(mixed[:, part(head)]).astype(jnp.bfloat16)


def on_device(
    mamba_input,
    mamba_gate,
    step_size,
    state_maps,
    decay_rate,
    skip_gain,
    norm_gain,
    queries,
    keys,
    values,
    source_len,
):
    segments = lax.axis_size("segment")
    ctx = lax.axis_size("ctx")
    tps = lax.axis_size("tp")
    index = lax.axis_index("ctx")
    index_in = index.astype(jnp.int32).reshape(1)
    onward = [(i, (i + 1) % segments) for i in range(segments)]
    partner = [(i, i + 1 - 2 * (i % 2)) for i in range(ctx)]
    further = [(i, (i + 2) % ctx) for i in range(ctx)]
    bf16, f32 = jnp.bfloat16, jnp.float32
    shape = jax.ShapeDtypeStruct

    def hand(array):
        return lax.ppermute(array, "segment", onward)

    def after(value, *others):
        return lax.optimization_barrier((value, *others))[0]

    x, gate, maps = mamba_input[0], mamba_gate[0], state_maps[0]
    dt = step_size[0].T
    heads, rows = dt.shape
    channels = x.shape[1]
    half = heads // 2
    side = channels // 2
    width = side // CHUNKS
    wire = bf16 if ctx <= 8 else f32
    groups = keys.shape[2] // HEAD_WIDTH
    wide = GROUP * HEAD_WIDTH

    whole = lambda *dims: pl.BlockSpec(dims, lambda i, s: (0,) * len(dims))
    fixed = lambda dims, *at: pl.BlockSpec(dims, lambda i, s: at)
    columns = lambda chunk: pl.BlockSpec(
        (rows, width), lambda i, s: (0, (s[0] % 2) * CHUNKS + chunk)
    )
    others = lambda chunk: pl.BlockSpec(
        (rows, width), lambda i, s: (0, (1 - s[0] % 2) * CHUNKS + chunk)
    )

    def indexed(kernel, out_shape, flops, nbytes, in_specs, out_specs, scratch=(), vmem=VMEM):
        return pl.pallas_call(
            kernel,
            out_shape=out_shape,
            grid_spec=pltpu.PrefetchScalarGridSpec(
                num_scalar_prefetch=1,
                grid=(1,),
                in_specs=in_specs,
                out_specs=out_specs,
                scratch_shapes=scratch,
            ),
            compiler_params=pltpu.CompilerParams(vmem_limit_bytes=vmem),
            cost_estimate=pl.CostEstimate(flops=flops, bytes_accessed=nbytes, transcendentals=0),
        )

    parcel_width = width + 2 * NST + rows
    hbm = pl.BlockSpec(memory_space=pltpu.HBM)
    kv_width = 2 * groups * HEAD_WIDTH
    *parcels, packed, rate, skip = indexed(
        parcel_kernel,
        (shape((rows, parcel_width), bf16),)
        + (shape((rows, width), bf16),) * (CHUNKS - 1)
        + (shape((rows, kv_width), bf16),)
        + (shape((1, heads), f32),) * 2,
        0,
        4 * rows * side,
        [hbm] * 7,
        (whole(rows, parcel_width),)
        + (whole(rows, width),) * (CHUNKS - 1)
        + (whole(rows, kv_width),)
        + (whole(1, heads),) * 2,
        [pltpu.SemaphoreType.DMA((CHUNKS + 6,))],
        PARCEL_VMEM,
    )(
        index_in,
        x,
        maps,
        dt,
        keys[0],
        values[0],
        decay_rate.reshape(1, heads),
        skip_gain.reshape(1, heads),
    )
    got = [lax.ppermute(parcels[0], "ctx", partner)]
    key_values = hand(packed)
    source = hand(source_len)
    x_own, maps_own, dt_own = indexed(
        load_kernel,
        (shape((rows, side), bf16), shape((rows, 2 * NST), bf16), shape((half, rows), bf16)),
        0,
        4 * rows * side,
        [hbm] * 3,
        (whole(rows, side), whole(rows, 2 * NST), whole(half, rows)),
        [pltpu.SemaphoreType.DMA((3,))],
        VMEM,
    )(after(index_in, parcels[0]), x, maps, dt)
    query = hand(after(queries[0], key_values, got[0], source, x_own))
    pairs = [
        lambda chunk: fixed((rows, width), 0, chunk),
        lambda chunk: whole(rows, width),
        lambda chunk: whole(half, rows),
        lambda chunk: fixed((half, rows), 0, (width + 2 * NST) // rows),
        lambda chunk: whole(1, heads),
    ]
    places = lambda chunk: [spec(chunk) for spec in pairs]
    states, firsts, leads, inner = [], [], [], []
    for chunk in range(CHUNKS):
        state, first, lead, both = indexed(
            functools.partial(state_kernel, chunk),
            (shape((NST, width), wire), shape((NST, width), f32)) + (shape((1, width), f32),) * 2,
            4 * rows * NST * width,
            4 * rows * width,
            places(chunk) + [whole(rows, NST), fixed((rows, NST), 0, width // NST)],
            (whole(NST, width),) * 2 + (whole(1, width),) * 2,
        )(index_in, x_own, got[chunk], dt_own, got[0], rate, maps_own, got[0])
        enter = lax.ppermute(state, "ctx", further)
        for _ in range(ctx // 2 - 2):
            enter = jnp.where(index < 2, 0.0, enter.astype(f32))
            enter = lax.ppermute((state.astype(f32) + both * enter).astype(wire), "ctx", further)
        states.append(enter)
        firsts.append(first)
        if chunk + 1 < CHUNKS:
            got.append(lax.ppermute(after(parcels[chunk + 1], first), "ctx", partner))
        leads.append(lead)
    for chunk in range(CHUNKS):
        inner.append(
            indexed(
                functools.partial(inner_kernel, chunk),
                (shape((rows, width), f32),) * 4,
                8 * rows * rows * width,
                6 * rows * width,
                places(chunk)
                + [
                    whole(1, heads),
                    whole(rows, 2 * NST),
                    fixed((rows, 2 * NST), 0, width // (2 * NST)),
                ],
                (whole(rows, width),) * 4,
            )(index_in, x_own, got[chunk], dt_own, got[0], rate, skip, maps_own, got[0])
        )
    scalar = pl.BlockSpec(memory_space=pltpu.SMEM)


    nearby = lax.ppermute(after(key_values, inner[0][0]), "ctx", partner)
    pieces, offsets = [key_values], [0]
    step = ctx // 2
    while step > 1:
        swap = [(i, i ^ step) for i in range(ctx)]
        pieces = pieces + [
            lax.ppermute(after(piece, states[0]), "ctx", swap) for piece in pieces
        ]
        offsets = offsets + [offset ^ step for offset in offsets]
        step //= 2
    far_pieces = pieces[1:] + [lax.ppermute(piece, "ctx", partner) for piece in pieces[1:]]
    far_offsets = offsets[1:] + [offset ^ 1 for offset in offsets[1:]]

    def attend(query, pieces, offsets, more, out_shape, out_specs):
        spots = lambda first: pl.BlockSpec((rows, HEAD_WIDTH), lambda g: (0, first + g))
        return call(
            functools.partial(attention_kernel, offsets),
            out_shape,
            4 * rows * wide * groups * len(offsets) * rows,
            8 * rows * wide * groups,
            VMEM + 8 * len(offsets) * rows * GROUP * rows,
            grid=(groups,),
            in_specs=[scalar, scalar, pl.BlockSpec((rows, wide), lambda g: (0, g))]
            + [spots(0)] * len(offsets)
            + [spots(groups)] * len(offsets)
            + (halves if more else []),
            out_specs=out_specs,
            scratch_shapes=[pltpu.VMEM((len(offsets) * rows, rows), f32)],
        )(index_in, source, query, *pieces, *pieces, *more)

    halves = [
        pl.BlockSpec((1, HEAD_WIDTH, GROUP * rows), lambda g: (g, 0, 0)),
        pl.BlockSpec((1, 2, GROUP * rows), lambda g: (g, 0, 0)),
    ]
    gated, sums, back = [], [], []
    for chunk in range(CHUNKS):
        some, part, away = indexed(
            outer_kernel,
            (shape((rows, width), bf16), shape((8, rows), f32), shape((rows, width), bf16)),
            4 * rows * rows * width,
            8 * rows * width,
            [whole(NST, width)] * 2
            + [whole(1, width)]
            + [whole(rows, width)] * 4
            + [
                fixed((rows, NST), 0, 1),
                fixed((rows, NST), 0, width // NST + 1),
                columns(chunk),
            ],
            (whole(rows, width), whole(8, rows), whole(rows, width)),
        )(index_in, after(states[chunk], query, nearby) if chunk else after(states[chunk], *[part for parts in inner for part in parts]), firsts[chunk], leads[chunk], *inner[chunk], maps_own, got[0], gate)
        gated.append(hand(some))
        sums.append(part)
        back.append(lax.ppermute(away, "ctx", partner))
    near = attend(
        after(query, some),
        [key_values, nearby],
        [0, 1],
        (),
        (
            shape((groups, HEAD_WIDTH, GROUP * rows), f32),
            shape((groups, 2, GROUP * rows), f32),
        ),
        tuple(halves),
    )
    for chunk in range(CHUNKS):
        some, part = indexed(
            gate_kernel,
            (shape((rows, width), bf16), shape((8, rows), f32)),
            2 * rows * width,
            8 * rows * width,
            [whole(rows, width), others(chunk)],
            (whole(rows, width), whole(8, rows)),
        )(index_in, after(back[chunk], gated[0], gated[1], *near), gate)
        gated.append(hand(some))
        sums.append(part)
    attention = attend(
        after(query, some, *gated[:3]),
        far_pieces,
        far_offsets,
        near,
        shape((rows, groups * wide), bf16),
        pl.BlockSpec((rows, wide), lambda g: (0, g)),
    )
    sums = sum(sums)
    swap = [(i, (i + step) % tps) for step in range(1, tps) for i in range(tps)]
    sums = hand(sums + lax.ppermute(sums, "tp", swap))

    mamba = indexed(
        functools.partial(norm_kernel, channels * tps),
        shape((rows, channels), bf16),
        rows * channels,
        4 * rows * channels,
        [whole(rows, width)] * (2 * CHUNKS) + [whole(8, rows), whole(1, channels)],
        whole(rows, channels),
    )(index_in, *gated, sums, norm_gain.reshape(1, channels))
    return (mamba[None], attention[None])


def solution(mesh):
    placed = (
        P("segment", "ctx", "tp"),
        P("segment", "ctx", "tp"),
        P("segment", "ctx", "tp"),
        P("segment", "ctx", None),
        P("tp"),
        P("tp"),
        P("tp"),
        P("segment", "ctx", "tp"),
        P("segment", "ctx", "tp"),
        P("segment", "ctx", "tp"),
        P("segment"),
    )
    return jax.shard_map(
        on_device,
        mesh=mesh,
        in_specs=placed,
        out_specs=(P("segment", "ctx", "tp"), P("segment", "ctx", "tp")),
        check_vma=False,
    )
```
